128 devices in a mesh: wide: 16 (over x, y), narrow: 8 (over z, core).
Axes of the slice: x: 4, y: 4, z: 4, core: 2. Of those that a mesh axis runs over, the one named last changes fastest.
Arguments:
- source: float32 [125, 131072], P(None, ('wide', 'narrow')), may hold values from -6 to 6
- inverses: float32 [4, 125, 125], replicated, may hold values from -0.3 to 2.3, as said below
- lift: float32 [125, 150], replicated, may hold values from -0.5 to 0.5
- stab: float32 [4], replicated, may hold values from 1 to 4
- material: int32 [131072], P(('wide', 'narrow')), may hold values from 0 to 3
- face_slot: int32 [6, 131072], P(None, ('wide', 'narrow')), may hold values from 0 to 3839, as said below
- owner_map: int32 [128, 768], P(('wide', 'narrow')), may hold values from 0 to 3072, as said below
Outputs:
- potential: float32 [125, 131072], P(None, ('wide', 'narrow'))
- trace_own: float32 [25, 393216], P(None, ('wide', 'narrow'))
The draws below stay inside these ranges and needn't reach their ends.
Inputs may be any that keep to these rules, and one draw needn't show every extreme that they name: `face_slot`: values below 3072 are faces the device owns, each named by some element of the device; 3072 + g is ghost slot g, named at most once and only where the neighbour's owner_map names it; a device holds at most 256 faces from a neighbour along the gap length and 128 across, both reached. `owner_map`: entry j of segment k of device d is the owned face that the neighbour of segment k holds in slot j of the opposite segment, or 3072 where it holds none; the faces named on one device are distinct. `inverses`: symmetric with a positive diagonal.
All inputs are finite; a program needn't handle non-finite values.
Results may differ from the reference program's by a relative error of at most 0.0001.
Values sent between devices are 32-bit elements; how exact they have to be, the bound alone decides.
A program may use at most 64 MiB of HBM per device.

```python
import math
import jax
import jax.numpy as jnp
from jax import lax

NODES = 125
FNODES = 25
TRACE = 150
MATS = 4
SWEEPS = 3
ELEM_DEV = 1024
CAP_W = 256
CAP_N = 128
GHOSTS = 768
ELEMS = 131072
FACES = 393216
N_WIDE = 16
N_NARROW = 8


def segment_layout():
    ghost_ids = jnp.arange(GHOSTS, dtype=jnp.int32)
    segment = (ghost_ids >= CAP_W).astype(jnp.int32) + (ghost_ids >= 2 * CAP_W).astype(jnp.int32) + (ghost_ids >= 2 * CAP_W + CAP_N).astype(jnp.int32)
    starts = jnp.array([0, CAP_W, 2 * CAP_W, 2 * CAP_W + CAP_N], jnp.int32)
    return (ghost_ids, segment, ghost_ids - starts[segment])


def neighbour_exists():
    device = jnp.arange(N_WIDE * N_NARROW, dtype=jnp.int32)
    wide_pos = device // N_NARROW
    narrow_pos = device % N_NARROW
    return jnp.stack([wide_pos > 0, wide_pos < N_WIDE - 1, narrow_pos > 0, narrow_pos < N_NARROW - 1], axis=1)


def neighbour_counts(key):
    devices = N_WIDE * N_NARROW
    device = jnp.arange(devices, dtype=jnp.int32)
    capacity = jnp.array([CAP_W, CAP_W, CAP_N, CAP_N], jnp.int32)
    key_count, key_offset = jax.random.split(key)
    counts = jax.random.randint(key_count, (devices, 4), capacity[None, :] // 2, capacity[None, :] + 1)
    offset_draw = jax.random.randint(key_offset, (), 0, 4)
    forced = (device + offset_draw) % 4
    counts = jnp.where(jnp.arange(4, dtype=jnp.int32)[None, :] == forced[:, None], capacity[None, :], counts)
    return jnp.where(neighbour_exists(), counts, 0)


def shuffle_one(one_key):
    return jax.random.permutation(one_key, 6 * ELEM_DEV)


def first_faces(one_key):
    return jax.random.permutation(one_key, 3 * ELEM_DEV)[:GHOSTS]


def draw_face_slot(key, part):
    counts = neighbour_counts(key)
    key = jax.random.fold_in(key, 11)
    devices = N_WIDE * N_NARROW
    owned_count = 3 * ELEM_DEV
    slots = 6 * ELEM_DEV
    ghost_ids, segment, column = segment_layout()
    valid = column[None, :] < counts[:, segment]
    key_fill, key_extra, key_order = jax.random.split(key, 3)
    filler = jax.random.randint(key_fill, (devices, GHOSTS), 0, owned_count)
    ghost_part = jnp.where(valid, owned_count + ghost_ids[None, :], filler)
    extra_faces = jax.random.randint(key_extra, (devices, slots - owned_count - GHOSTS), 0, owned_count)
    each_face = jnp.broadcast_to(jnp.arange(owned_count, dtype=jnp.int32)[None, :], (devices, owned_count))
    layout = jnp.concatenate([each_face, ghost_part, extra_faces], axis=1).astype(jnp.int32)
    orders = jax.vmap(shuffle_one)(jax.random.split(key_order, devices))
    shuffled = jnp.take_along_axis(layout, orders, axis=1)
    return shuffled.reshape(devices, 6, ELEM_DEV).transpose(1, 0, 2).reshape(6, devices * ELEM_DEV)


def draw_owner_map(key, part):
    counts = neighbour_counts(key)
    key = jax.random.fold_in(key, 12)
    devices = N_WIDE * N_NARROW
    owned_count = 3 * ELEM_DEV
    ghost_ids, segment, column = segment_layout()
    device = jnp.arange(devices, dtype=jnp.int32)[:, None]
    wide_step = jnp.array([-1, 1, 0, 0], jnp.int32)
    narrow_step = jnp.array([0, 0, -1, 1], jnp.int32)
    opposite = jnp.array([1, 0, 3, 2], jnp.int32)
    wide_pos = jnp.clip(device // N_NARROW + wide_step[segment][None, :], 0, N_WIDE - 1)
    narrow_pos = jnp.clip(device % N_NARROW + narrow_step[segment][None, :], 0, N_NARROW - 1)
    neighbour = wide_pos * N_NARROW + narrow_pos
    their_count = counts[neighbour, opposite[segment][None, :]]
    valid = neighbour_exists()[:, segment] & (column[None, :] < their_count)
    picks = jax.vmap(first_faces)(jax.random.split(key, devices)).astype(jnp.int32)
    return jnp.where(valid, picks, owned_count).astype(jnp.int32)


def draw_inverses(key, part):
    key = jax.random.fold_in(key, 13)
    key_diag, key_off = jax.random.split(key)
    diagonal = jax.random.uniform(key_diag, (MATS, NODES), jnp.float32, 1.0, 2.0)
    spread = jnp.clip(0.04 * jax.random.normal(key_off, (MATS, NODES, NODES), jnp.float32), -0.2, 0.2)
    mixed_part = (spread + jnp.swapaxes(spread, 1, 2)) * 0.7071
    return mixed_part + diagonal[:, :, None] * jnp.eye(NODES, dtype=jnp.float32)[None, :, :]


def plant(values, stream_key, smallest, high):
    place = [jax.random.randint(jax.random.fold_in(stream_key, axis), (), 0, length) for axis, length in enumerate(values.shape)]
    widest = values.shape.index(max(values.shape))
    beside = place[:widest] + [(place[widest] + 1) % values.shape[widest]] + place[widest + 1:]
    return values.at[tuple(place)].set(smallest).at[tuple(beside)].set(high)


def level_of(own_key, extent, shards, low, largest):
    def one(position, parts):
        steps = jax.random.uniform(jax.random.fold_in(jax.random.fold_in(own_key, 6), position), (parts,), jnp.float32, low / len(shards), largest / len(shards))
        return jnp.repeat(jnp.exp(steps), extent[position] // parts).reshape((-1,) + (1,) * (len(extent) - position - 1))

    loudness = one(*shards[0])
    for cut in shards[1:]:
        loudness = loudness * one(*cut)
    return loudness


def centred(own_key, dims, width, reach, cuts=(), kind=jnp.bfloat16):
    drawn = width * jax.random.normal(own_key, dims, jnp.float32)
    if cuts:
        drawn = drawn * level_of(own_key, dims, cuts, -0.22, 0.18)
    return jnp.clip(drawn, -reach, reach).astype(kind)


def setup_inputs(seed: int = 0) -> dict:
    splits = jax.random.split(jax.random.key(seed), 8)
    source = centred(splits[0], (NODES, ELEMS), 1.0, 6.0, ((1, 128),), jnp.float32)
    inverses = draw_inverses(jax.random.fold_in(splits[7], 71), 0)
    lift = centred(splits[2], (NODES, TRACE), NODES ** -0.5, 0.5, (), jnp.float32)
    stab = jnp.clip(jnp.exp(jax.random.uniform(splits[3], (MATS,), jnp.float32, math.log(1.0), math.log(4.0))), 1.0, 4.0)
    material = plant(jax.random.randint(splits[4], (ELEMS,), 0, MATS), jax.random.fold_in(splits[4], 1), 0, MATS - 1).astype(jnp.int32)
    face_slot = draw_face_slot(jax.random.fold_in(splits[7], 71), 0)
    owner_map = draw_owner_map(jax.random.fold_in(splits[7], 71), 0)
    return dict(source=source, inverses=inverses, lift=lift, stab=stab, material=material, face_slot=face_slot, owner_map=owner_map)


HIGH = lax.Precision.HIGHEST
damping = 0.6


def per_material(inverses, material, values):
    result = jnp.zeros(values.shape, jnp.float32)
    for mat_id in range(inverses.shape[0]):
        product = jnp.dot(inverses[mat_id], values, precision=HIGH, preferred_element_type=jnp.float32)
        result = result + jnp.where(material[None, :] == mat_id, product, jnp.float32(0.0))
    return result


def per_element(table_rows, material):
    result = jnp.zeros((table_rows.shape[1], material.shape[0]), jnp.float32)
    for mat_id in range(table_rows.shape[0]):
        result = result + jnp.where(material[None, :] == mat_id, table_rows[mat_id][:, None], jnp.float32(0.0))
    return result


def trace_diagonal(inverses, lift, stab):
    applied = jnp.einsum("mij,jt->mit", inverses, lift, precision=HIGH)
    return stab[:, None] + jnp.abs(jnp.sum(lift[None, :, :] * applied, axis=1))


def element_terms(values, lift, inverses, material, stab_cols):
    lifted = jnp.dot(lift, values, precision=HIGH, preferred_element_type=jnp.float32)
    solved = per_material(inverses, material, lifted)
    return stab_cols * values + jnp.dot(lift.T, solved, precision=HIGH, preferred_element_type=jnp.float32)


def global_faces(face_slot, owner_map):
    elem_count = face_slot.shape[1]
    owned_count = 3 * ELEM_DEV
    device = (jnp.arange(elem_count, dtype=jnp.int32) // ELEM_DEV)[None, :]
    ghost_index = face_slot - owned_count
    segment = (ghost_index >= CAP_W).astype(jnp.int32) + (ghost_index >= 2 * CAP_W).astype(jnp.int32) + (ghost_index >= 2 * CAP_W + CAP_N).astype(jnp.int32)
    starts = jnp.array([0, CAP_W, 2 * CAP_W, 2 * CAP_W + CAP_N], jnp.int32)
    far_starts = jnp.array([CAP_W, 0, 2 * CAP_W + CAP_N, 2 * CAP_W], jnp.int32)
    wide_step = jnp.array([-1, 1, 0, 0], jnp.int32)
    narrow_step = jnp.array([0, 0, -1, 1], jnp.int32)
    column = ghost_index - starts[segment]
    wide_pos = jnp.clip(device // N_NARROW + wide_step[segment], 0, N_WIDE - 1)
    narrow_pos = jnp.clip(device % N_NARROW + narrow_step[segment], 0, N_NARROW - 1)
    neighbour = (wide_pos * N_NARROW + narrow_pos).astype(jnp.int32)
    far_column = jnp.clip(far_starts[segment] + column, 0, GHOSTS - 1).astype(jnp.int32)
    remote = neighbour * owned_count + owner_map[neighbour, far_column]
    return jnp.where(ghost_index < 0, device * owned_count + face_slot, remote).astype(jnp.int32)


def assemble(terms, face_ids):
    flat_terms = terms.reshape(FNODES, -1)
    return jnp.zeros((FNODES, FACES), jnp.float32).at[:, face_ids.reshape(-1)].add(flat_terms)


def element_values(trace_table, face_ids):
    return trace_table[:, face_ids].reshape(FNODES * 6, face_ids.shape[1])


def reference(source, inverses, lift, stab, material, face_slot, owner_map):
    face_ids = global_faces(face_slot, owner_map)
    base_state = per_material(inverses, material, source)
    rhs = assemble(jnp.dot(lift.T, base_state, precision=HIGH, preferred_element_type=jnp.float32), face_ids)
    diag = assemble(per_element(trace_diagonal(inverses, lift, stab), material), face_ids)
    stab_cols = per_element(stab[:, None], material)
    trace_own = damping * rhs / diag
    for sweep_index in range(SWEEPS - 1):
        terms = element_terms(element_values(trace_own, face_ids), lift, inverses, material, stab_cols)
        applied = assemble(terms, face_ids)
        trace_own = trace_own + damping * (rhs - applied) / diag
    lifted = jnp.dot(lift, element_values(trace_own, face_ids), precision=HIGH, preferred_element_type=jnp.float32)
    potential = base_state - per_material(inverses, material, lifted)
    return potential, trace_own
```

```python
import functools

import jax
import jax.numpy as jnp
from jax import lax
from jax.experimental import pallas as pl
from jax.experimental.pallas import tpu as pltpu
from jax.sharding import PartitionSpec as P

MESH = pl.DeviceIdType.MESH
F32, BF = jnp.float32, jnp.bfloat16
HIGH = lax.Precision.HIGHEST
DAMPING = 0.6
SWEEPS = 3

NODES, FNODES, SIDES, MATS = 125, 25, 6, 4
ELEM = 1024
OWNED = 3 * ELEM
CAP_W, CAP_N = 256, 128
GHOSTS = 2 * CAP_W + 2 * CAP_N
TP = 160
NP = 128

OWN_BLOCKS, BLOCKS = 12, 18
OWN_MAIN, OWN_LEFT, OUT_MAIN, OUT_LEFT, ROWS = 0, 288, 304, 448, 464
GROUPS = {
    "own": (0, 12, OWN_MAIN, OWN_LEFT),
    "out": (12, 18, OUT_MAIN, OUT_LEFT),
}
SENT = 56
ROUNDS = 2 + SWEEPS - 1


def dot(a, b, precision=None):
    return jnp.dot(a, b, precision=precision, preferred_element_type=F32)


def dot_nt(a, b, precision=None):
    return lax.dot_general(
        a, b, (((1,), (1,)), ((), ())), precision=precision, preferred_element_type=F32
    )


def split(x):
    hi = x.astype(BF)
    return hi, (x - hi.astype(F32)).astype(BF)


def iota(shape, dim):
    return lax.broadcasted_iota(jnp.int32, shape, dim)


def trace_position(p):
    side = jnp.zeros_like(p)
    for i in range(1, SIDES):
        side = side + (p >= 24 * i).astype(jnp.int32)
    node = jnp.where(p < 144, p - 24 * side, 24)
    side = jnp.where(p < 144, side, p - 144)
    return side, node


def kernel(
    source, inverses, lift, stab, material, face_slot, owner_map,
    potential, trace_own,
    onehot, onehot_out, blk_f, blk_d, idx_f, counts,
    inv_pad, lift_pad, src_pad, src3, left3, a3, w3,
    rhs_terms, x_main, x_left, x3, t_hi, t_lo, l_hi, l_lo,
    partial, total, table, table2, scale,
    send_w, recv_w, send_n, recv_n, send_sems, recv_sems,
):
    w, n = lax.axis_index("wide"), lax.axis_index("narrow")
    wide, narrow = lax.axis_size("wide"), lax.axis_size("narrow")
    there = (w > 0, w < wide - 1, n > 0, n < narrow - 1)
    neighbour = ((w - 1, n), (w + 1, n), (w, n - 1), (w, n + 1))
    barrier = pltpu.get_barrier_semaphore()
    present = jnp.int32(0)
    for k in range(4):
        present = present + there[k].astype(jnp.int32)

        @pl.when(there[k])
        def _():
            pl.semaphore_signal(barrier, inc=1, device_id=neighbour[k], device_id_type=MESH)

    pl.semaphore_wait(barrier, present)

    def buffers(k):
        return (send_w, recv_w, k) if k < 2 else (send_n, recv_n, k - 2)

    for k in range(4):
        send, recv, side = buffers(k)

        @pl.when(jnp.logical_not(there[k]))
        def _():
            for r in range(ROUNDS):
                recv[r, side] = jnp.zeros(recv.shape[2:], F32)

    def copy(r, k):
        send, recv, side = buffers(k)
        return pltpu.make_async_remote_copy(
            src_ref=send.at[r, side],
            dst_ref=recv.at[r, 1 - side],
            send_sem=send_sems.at[r, k],
            recv_sem=recv_sems.at[r, k ^ 1],
            device_id=neighbour[k],
            device_id_type=MESH,
        )

    def arrival(r, k):
        send, recv, side = buffers(k)
        return pltpu.make_async_remote_copy(
            src_ref=send.at[r, side],
            dst_ref=recv.at[r, side],
            send_sem=send_sems.at[r, k],
            recv_sem=recv_sems.at[r, k],
            device_id=neighbour[k],
            device_id_type=MESH,
        )

    def places(k):
        block = min(k, 2)
        lo, width = (0, CAP_W) if k < 2 else ((k - 2) * CAP_N, CAP_N)
        return block, slice(lo, lo + width)

    def post(r, values):
        for k in range(4):
            send, recv, side = buffers(k)
            block, cols = places(k)
            ghost, shared = OUT_MAIN + 24 * block, OUT_MAIN + 24 * (block + 3)
            send[r, side, 0:24] = values[ghost : ghost + 24, cols]
            send[r, side, 24:48] = values[shared : shared + 24, cols]
            ghost, shared = OUT_LEFT + block, OUT_LEFT + block + 3
            send[r, side, 48:49] = values[ghost : ghost + 1, cols]
            send[r, side, 49:50] = values[shared : shared + 1, cols]

            @pl.when(there[k])
            def _():
                copy(r, k).start()

    def collect(r, values):
        for k in range(4):
            @pl.when(there[k])
            def _():
                arrival(r, k).wait_recv()

        for k in range(4):
            send, recv, side = buffers(k)
            block, cols = places(k)
            ghost, shared = OUT_MAIN + 24 * block, OUT_MAIN + 24 * (block + 3)
            values[shared : shared + 24, cols] += recv[r, side, 0:24]
            values[ghost : ghost + 24, cols] += recv[r, side, 24:48]
            ghost, shared = OUT_LEFT + block, OUT_LEFT + block + 3
            values[shared : shared + 1, cols] += recv[r, side, 48:49]
            values[ghost : ghost + 1, cols] += recv[r, side, 49:50]

    owners = owner_map[...]
    own_blk, own_col = owners >> 8, owners & 255
    place = iota((1, GHOSTS), 1) + 1
    onehot_out[...] = (iota((256, GHOSTS), 0) == own_col).astype(F32).astype(BF)
    row16 = iota((16, GHOSTS), 0)
    named = jnp.where(row16 < OWN_BLOCKS, row16, -1) == own_blk
    digits = jnp.concatenate(
        [
            jnp.where(named, (place >> 8).astype(F32), 0.0),
            jnp.where(named, (place & 255).astype(F32), 0.0),
        ],
        axis=0,
    ).astype(BF)
    place_table = dot_nt(digits, onehot_out[...]).astype(BF)

    def renumber(s, carry):
        v = face_slot[pl.ds(s, 1), :]
        col = jnp.broadcast_to(v & 255, (256, ELEM))
        first = (iota((256, ELEM), 0) == col).astype(F32).astype(BF)
        found = dot(place_table, first)
        hit = iota((16, ELEM), 0) == (v >> 8)
        spot = jnp.sum(
            jnp.where(hit, 256.0 * found[0:16] + found[16:32], 0.0), axis=0, keepdims=True
        ).astype(jnp.int32)
        v = jnp.where(spot > 0, OWNED + GHOSTS - 1 + spot, v)
        onehot[s] = (iota((256, ELEM), 0) == (v & 255)).astype(F32).astype(BF)
        blk = (v >> 8).astype(F32)
        blk_f[s] = jnp.broadcast_to(blk, (8, ELEM))
        blk_d[s] = (blk - (iota((48, ELEM), 0) >= 24).astype(F32)).astype(BF)
        idx = 8.0 * blk + material[...].astype(F32)
        idx_f[s] = (idx - iota((16, ELEM), 0).astype(F32)).astype(BF)
        return carry

    lax.fori_loop(0, SIDES, renumber, 0)

    def count(s, carry):
        idx = idx_f[s]
        ones = jnp.concatenate(
            [
                jnp.where(idx == BF(16 * t), BF(1), BF(0))
                for t in range(8 * BLOCKS // 16)
            ],
            axis=0,
        )
        counts[s] = dot_nt(ones, onehot[s])
        return carry

    lax.fori_loop(0, SIDES, count, 0)

    inv_pad[...] = jnp.zeros_like(inv_pad)
    inv_pad[:, 0:NODES, 0:NODES] = inverses[...]
    lift_pad[...] = jnp.zeros_like(lift_pad)
    lift_pad[0:NODES, 0 : SIDES * FNODES] = lift[...]
    src_pad[...] = jnp.zeros_like(src_pad)
    src_pad[0:NODES] = source[...]
    hi, lo = split(src_pad[...])
    src3[0:NP], src3[NP : 2 * NP], src3[2 * NP :] = hi, lo, hi

    side_p, node_p = trace_position(iota((TP, 256), 0))
    order = jnp.where(side_p < SIDES, 6 * node_p + side_p, -1)
    perm = (iota((TP, 256), 1) == order).astype(F32)
    lift_t = dot_nt(perm, lift_pad[...], HIGH)
    lift_p = dot_nt(lift_pad[...], perm, HIGH)
    eye = iota((TP, TP), 0) == iota((TP, TP), 1)
    col = iota((TP, 192), 1)
    for i in range(1, 4):
        col = col - 48 * (iota((TP, 192), 1) >= 48 * i).astype(jnp.int32)
    side_c, _ = trace_position(iota((TP, 192), 0))
    spread = jnp.zeros((TP, 192), F32)
    for m in range(MATS):
        inv = inv_pad[m]
        wm = dot(inv, lift_p, HIGH)
        wt = dot(lift_t, inv, HIGH)
        am = dot(wt, lift_p, HIGH)
        diagonal = jnp.abs(jnp.sum(jnp.where(eye, am, 0.0), axis=1, keepdims=True)) + stab[m]
        spread = spread + jnp.where(col == 8 * side_c + m, diagonal, 0.0)
        am = am + jnp.where(eye, stab[m], 0.0)
        hi, lo = split(am)
        a3[TP * m : TP * (m + 1)] = jnp.concatenate([hi, hi, lo], axis=1)
        hi, lo = split(wm)
        w3[NP * m : NP * (m + 1)] = jnp.concatenate([hi, hi, lo], axis=1)
        hi, lo = split(wt)
        r = slice(TP * m, TP * (m + 1))
        left3[r, 0:NP], left3[r, NP : 2 * NP], left3[r, 2 * NP :] = hi, hi, lo
        hi, lo = split(inv)
        r = slice(MATS * TP + NP * m, MATS * TP + NP * (m + 1))
        left3[r, 0:NP], left3[r, NP : 2 * NP], left3[r, 2 * NP :] = hi, hi, lo
    sdiag = jnp.zeros((24, 192), F32)
    for s in range(SIDES):
        sdiag = sdiag + spread[24 * s : 24 * s + 24]
    last = jnp.sum(spread[144:152], axis=0, keepdims=True)
    sdiag = jnp.concatenate([sdiag, jnp.broadcast_to(last, (8, 192))], axis=0)
    hi = sdiag.astype(BF).astype(F32)
    sdiag = jnp.where(iota((32, 192), 1) < 96, hi, sdiag - hi).astype(BF)

    def diag_block(a):
        _, _, main, left = GROUPS["own" if a < OWN_BLOCKS else "out"]
        b = a if a < OWN_BLOCKS else a - OWN_BLOCKS
        met = jnp.concatenate([counts[s, 8 * a : 8 * a + 8] for s in range(SIDES)], axis=0)
        hi, lo = split(met)
        d = dot(sdiag, jnp.concatenate([hi, lo, hi, lo], axis=0))
        scale[main + 24 * b : main + 24 * b + 24] = d[0:24]
        scale[left + b : left + b + 1] = d[24:25]

    scale[...] = jnp.zeros_like(scale)
    for a in range(OWN_BLOCKS, BLOCKS):
        diag_block(a)
    post(0, scale)

    mat = material[...]

    def pick(y, width, e):
        m_row = jnp.broadcast_to(mat[:, e], (8, y.shape[1]))[None]
        y = y.reshape(MATS, width // 8, 8, y.shape[1])
        return jnp.where(
            m_row == 0, y[0], jnp.where(m_row == 1, y[1], jnp.where(m_row == 2, y[2], y[3]))
        ).reshape(width, y.shape[3])

    CHUNK = 512
    for c in range(ELEM // CHUNK):
        e = slice(c * CHUNK, (c + 1) * CHUNK)
        y = dot(left3[...], src3[:, e])
        rhs_terms[:, e] = pick(y[0 : MATS * TP], TP, e)
        potential[:, e] = pick(y[MATS * TP :], NP, e)[0:NODES]

    def store_terms(terms, e):
        for s in range(SIDES):
            t = terms[24 * s : 24 * s + 24]
            hi, lo = split(jnp.concatenate([t, t], axis=0))
            t_hi[s, :, e], t_lo[s, :, e] = hi, lo
            t = jnp.broadcast_to(terms[144 + s : 145 + s], (16, terms.shape[1]))
            hi, lo = split(t)
            l_hi[s, :, e], l_lo[s, :, e] = hi, lo

    for c in range(ELEM // CHUNK):
        e = slice(c * CHUNK, (c + 1) * CHUNK)
        store_terms(rhs_terms[:, e], e)

    def row_ids(first, last, dtype):
        r = iota((16, ELEM), 0)
        return jnp.where(r < last - first, r + first, -1).astype(F32).astype(dtype)

    def assemble(name):
        first, last, main, left = GROUPS[name]
        rows = slice(main, left + 16)
        partial[rows] = jnp.zeros((left + 16 - main, 256), F32)

        def add(s, carry):
            hit = row_ids(first, last, BF) == blk_d[s, 0:16]
            hits = [blk_d[s] == BF(a) for a in range(first, last, 2)]
            out = None
            for t, l in ((t_hi, l_hi), (t_lo, l_lo)):
                tv = t[s]
                z = jnp.concatenate(
                    [jnp.where(h, tv, BF(0)) for h in hits] + [jnp.where(hit, l[s], BF(0))], axis=0
                )
                d = dot_nt(z, onehot[s])
                out = d if out is None else out + d
            partial[rows] += out
            return carry

        lax.fori_loop(0, SIDES, add, 0)

    def fetch(name):
        first, last, main, left = GROUPS[name]

        def take(s, carry):
            y = dot(table[main : left + 16], onehot[s]) + dot(table2[main : left + 16], onehot[s])
            blk = blk_f[s]
            if name == "own":
                acc = jnp.zeros((3, 8, ELEM), F32)
                acc_left = jnp.zeros((1, ELEM), F32)
            else:
                acc = x_main[s].reshape(3, 8, ELEM)
                acc_left = x_left[s, 0:1]
            for a in range(first, last):
                ya = y[24 * (a - first) : 24 * (a - first) + 24].reshape(3, 8, ELEM)
                acc = jnp.where((blk == F32(a))[None], ya, acc)
            x_main[s] = acc.reshape(24, ELEM)
            hit = row_ids(first, last, F32).reshape(2, 8, ELEM) == blk[None]
            yl = jnp.where(hit, y[left - main :].reshape(2, 8, ELEM), 0.0)
            x_left[s, 0:1] = acc_left + jnp.sum(yl[0] + yl[1], axis=0, keepdims=True)
            return carry

        lax.fori_loop(0, SIDES, take, 0)

    def gathered():
        rows = [x_main[s] for s in range(SIDES)]
        x = jnp.concatenate([x_left[s, 0:1] for s in range(SIDES)] + [jnp.zeros((10, ELEM), F32)], axis=0)
        x = jnp.concatenate(rows + [x], axis=0)
        hi, lo = split(x)
        x3[0:TP], x3[TP : 2 * TP], x3[2 * TP :] = hi, lo, hi

    def table_rows(name):
        _, _, main, left = GROUPS[name]
        return slice(main, left + 16)

    def update(name, first):
        rows = table_rows(name)
        step = scale[rows] * partial[rows]
        x = step if first else total[rows] + step
        total[rows] = x
        hi, lo = split(x)
        table[rows], table2[rows] = hi, lo

    assemble("out")
    post(1, partial)
    for a in range(OWN_BLOCKS):
        diag_block(a)
    assemble("own")

    def invert(name):
        rows = table_rows(name)
        d = scale[rows]
        scale[rows] = jnp.where(d == 0.0, 0.0, DAMPING / jnp.where(d == 0.0, 1.0, d))

    invert("own")
    update("own", True)
    fetch("own")
    collect(0, scale)
    collect(1, partial)
    invert("out")
    update("out", True)
    fetch("out")

    for sweep in range(SWEEPS - 1):
        gathered()
        for c in range(ELEM // CHUNK):
            e = slice(c * CHUNK, (c + 1) * CHUNK)
            y = pick(dot(a3[...], x3[:, e]), TP, e)
            store_terms(rhs_terms[:, e] - y, e)
        assemble("out")
        post(2 + sweep, partial)
        assemble("own")
        update("own", False)
        fetch("own")
        collect(2 + sweep, partial)
        update("out", False)
        fetch("out")

    rows = slice(OWN_MAIN, OWN_LEFT + 16)
    back = jnp.zeros((304, 256), F32)
    for b in range(3):
        cols = slice(256 * b, 256 * (b + 1))
        r = OUT_MAIN + 24 * (b + 3)
        x = total[r : r + 24]
        xl = jnp.broadcast_to(total[OUT_LEFT + b + 3 : OUT_LEFT + b + 4], (16, 256))
        blk = own_blk[:, cols].astype(F32)
        blk2 = (blk - (iota((48, 256), 0) >= 24).astype(F32)).astype(BF)
        hits = [blk2 == BF(a) for a in range(0, OWN_BLOCKS, 2)]
        r16 = iota((16, 256), 0)
        hit = jnp.where(r16 < OWN_BLOCKS, r16, -1).astype(F32).astype(BF) == blk.astype(BF)
        for xv, lv in zip(split(jnp.concatenate([x, x], axis=0)), split(xl)):
            z = jnp.concatenate(
                [jnp.where(h, xv, BF(0)) for h in hits] + [jnp.where(hit, lv, BF(0))], axis=0
            )
            back = back + dot_nt(z, onehot_out[:, cols])
    full = total[rows] + back
    for a in range(OWN_BLOCKS):
        cols = slice(256 * a, 256 * (a + 1))
        trace_own[0:24, cols] = full[24 * a : 24 * a + 24]
        trace_own[24:25, cols] = full[OWN_LEFT + a : OWN_LEFT + a + 1]

    gathered()
    for c in range(ELEM // CHUNK):
        e = slice(c * CHUNK, (c + 1) * CHUNK)
        y = pick(dot(w3[...], x3[:, e]), NP, e)
        potential[:, e] = potential[:, e] - y[0:NODES]

    for r in range(ROUNDS):
        for k in range(4):
            @pl.when(there[k])
            def _():
                copy(r, k).wait_send()


def shards(source, inverses, lift, stab, material, face_slot, owner_map):
    vmem = pl.BlockSpec(memory_space=pltpu.VMEM)
    smem = pl.BlockSpec(memory_space=pltpu.SMEM)
    v = pltpu.VMEM
    return pl.pallas_call(
        kernel,
        out_shape=(
            jax.ShapeDtypeStruct((NODES, ELEM), F32),
            jax.ShapeDtypeStruct((FNODES, OWNED), F32),
        ),
        in_specs=[vmem, vmem, vmem, smem, vmem, vmem, vmem],
        out_specs=(vmem, vmem),
        scratch_shapes=[
            v((SIDES, 256, ELEM), BF),
            v((256, GHOSTS), BF),
            v((SIDES, 8, ELEM), F32),
            v((SIDES, 48, ELEM), BF),
            v((SIDES, 16, ELEM), BF),
            v((SIDES, 8 * BLOCKS, 256), F32),
            v((MATS, NP, NP), F32),
            v((NP, 256), F32),
            v((NP, ELEM), F32),
            v((3 * NP, ELEM), BF),
            v((MATS * (TP + NP), 3 * NP), BF),
            v((MATS * TP, 3 * TP), BF),
            v((MATS * NP, 3 * TP), BF),
            v((TP, ELEM), F32),
            v((SIDES, 24, ELEM), F32),
            v((SIDES, 8, ELEM), F32),
            v((3 * TP, ELEM), BF),
            v((SIDES, 48, ELEM), BF),
            v((SIDES, 48, ELEM), BF),
            v((SIDES, 16, ELEM), BF),
            v((SIDES, 16, ELEM), BF),
            v((ROWS, 256), F32),
            v((ROWS, 256), F32),
            v((ROWS, 256), BF),
            v((ROWS, 256), BF),
            v((ROWS, 256), F32),
            v((ROUNDS, 2, SENT, CAP_W), F32),
            v((ROUNDS, 2, SENT, CAP_W), F32),
            v((ROUNDS, 2, SENT, CAP_N), F32),
            v((ROUNDS, 2, SENT, CAP_N), F32),
            pltpu.SemaphoreType.DMA((ROUNDS, 4)),
            pltpu.SemaphoreType.DMA((ROUNDS, 4)),
        ],
        compiler_params=pltpu.CompilerParams(
            collective_id=0, has_side_effects=True, vmem_limit_bytes=48 * 2**20
        ),
    )(source, inverses, lift, stab, material.reshape(1, ELEM), face_slot, owner_map)


def solution(mesh):
    both = ("wide", "narrow")
    return jax.shard_map(
        shards,
        mesh=mesh,
        in_specs=(
            P(None, both), P(), P(), P(), P(both), P(None, both), P(both, None),
        ),
        out_specs=(P(None, both), P(None, both)),
        check_vma=False,
    )
```

```python
import functools

import jax
import jax.numpy as jnp
from jax import lax
from jax.experimental import pallas as pl
from jax.experimental.pallas import tpu as pltpu
from jax.sharding import PartitionSpec as P

MESH = pl.DeviceIdType.MESH
F32, BF = jnp.float32, jnp.bfloat16
HIGH = lax.Precision.HIGHEST
DAMPING = 0.6
SWEEPS = 3

NODES, FNODES, SIDES, MATS = 125, 25, 6, 4
ELEM = 1024
OWNED = 3 * ELEM
CAP_W, CAP_N = 256, 128
GHOSTS = 2 * CAP_W + 2 * CAP_N
TP = 160
NP = 128

OWN_BLOCKS, BLOCKS = 12, 18
OWN_MAIN, OWN_LEFT, OUT_MAIN, OUT_LEFT, ROWS = 0, 288, 304, 448, 464
GROUPS = {
    "own": (0, 12, OWN_MAIN, OWN_LEFT),
    "out": (12, 18, OUT_MAIN, OUT_LEFT),
}
SENT = 56
ROUNDS = 2 + SWEEPS - 1


def dot(a, b, precision=None):
    return jnp.dot(a, b, precision=precision, preferred_element_type=F32)


def dot_nt(a, b, precision=None):
    return lax.dot_general(
        a, b, (((1,), (1,)), ((), ())), precision=precision, preferred_element_type=F32
    )


def split(x):
    hi = x.astype(BF)
    return hi, (x - hi.astype(F32)).astype(BF)


def iota(shape, dim):
    return lax.broadcasted_iota(jnp.int32, shape, dim)


def trace_position(p):
    side = jnp.zeros_like(p)
    for i in range(1, SIDES):
        side = side + (p >= 24 * i).astype(jnp.int32)
    node = jnp.where(p < 144, p - 24 * side, 24)
    side = jnp.where(p < 144, side, p - 144)
    return side, node


def kernel(
    source, inverses, lift, stab, material, face_slot, owner_map,
    potential, trace_own,
    onehot, onehot_out, blk_f, blk_d, idx_f, counts,
    inv_pad, lift_pad, src_pad, src3, left3, a3, w3,
    rhs_terms, x_main, x_left, x3, t_hi, t_lo, l_hi, l_lo,
    partial, total, table, table2, scale,
    send_w, recv_w, send_n, recv_n, send_sems, recv_sems,
):
    w, n = lax.axis_index("wide"), lax.axis_index("narrow")
    wide, narrow = lax.axis_size("wide"), lax.axis_size("narrow")
    there = (w > 0, w < wide - 1, n > 0, n < narrow - 1)
    neighbour = ((w - 1, n), (w + 1, n), (w, n - 1), (w, n + 1))
    barrier = pltpu.get_barrier_semaphore()
    present = jnp.int32(0)
    for k in range(4):
        present = present + there[k].astype(jnp.int32)

        @pl.when(there[k])
        def _():
            pl.semaphore_signal(barrier, inc=1, device_id=neighbour[k], device_id_type=MESH)

    pl.semaphore_wait(barrier, present)

    def buffers(k):
        return (send_w, recv_w, k) if k < 2 else (send_n, recv_n, k - 2)

    for k in range(4):
        send, recv, side = buffers(k)

        @pl.when(jnp.logical_not(there[k]))
        def _():
            for r in range(ROUNDS):
                recv[r, side] = jnp.zeros(recv.shape[2:], F32)

    def copy(r, k):
        send, recv, side = buffers(k)
        return pltpu.make_async_remote_copy(
            src_ref=send.at[r, side],
            dst_ref=recv.at[r, 1 - side],
            send_sem=send_sems.at[r, k],
            recv_sem=recv_sems.at[r, k ^ 1],
            device_id=neighbour[k],
            device_id_type=MESH,
        )

    def arrival(r, k):
        send, recv, side = buffers(k)
        return pltpu.make_async_remote_copy(
            src_ref=send.at[r, side],
            dst_ref=recv.at[r, side],
            send_sem=send_sems.at[r, k],
            recv_sem=recv_sems.at[r, k],
            device_id=neighbour[k],
            device_id_type=MESH,
        )

    def places(k):
        block = min(k, 2)
        lo, width = (0, CAP_W) if k < 2 else ((k - 2) * CAP_N, CAP_N)
        return block, slice(lo, lo + width)

    def post(r, values):
        for k in range(4):
            send, recv, side = buffers(k)
            block, cols = places(k)
            ghost, shared = OUT_MAIN + 24 * block, OUT_MAIN + 24 * (block + 3)
            send[r, side, 0:24] = values[ghost : ghost + 24, cols]
            send[r, side, 24:48] = values[shared : shared + 24, cols]
            ghost, shared = OUT_LEFT + block, OUT_LEFT + block + 3
            send[r, side, 48:49] = values[ghost : ghost + 1, cols]
            send[r, side, 49:50] = values[shared : shared + 1, cols]

            @pl.when(there[k])
            def _():
                copy(r, k).start()

    def collect(r, values):
        for k in range(4):
            @pl.when(there[k])
            def _():
                arrival(r, k).wait_recv()

        for k in range(4):
            send, recv, side = buffers(k)
            block, cols = places(k)
            ghost, shared = OUT_MAIN + 24 * block, OUT_MAIN + 24 * (block + 3)
            values[shared : shared + 24, cols] += recv[r, side, 0:24]
            values[ghost : ghost + 24, cols] += recv[r, side, 24:48]
            ghost, shared = OUT_LEFT + block, OUT_LEFT + block + 3
            values[shared : shared + 1, cols] += recv[r, side, 48:49]
            values[ghost : ghost + 1, cols] += recv[r, side, 49:50]

    owners = owner_map[...]
    own_blk, own_col = owners >> 8, owners & 255
    place = iota((1, GHOSTS), 1) + 1
    onehot_out[...] = (iota((256, GHOSTS), 0) == own_col).astype(F32).astype(BF)
    row16 = iota((16, GHOSTS), 0)
    named = jnp.where(row16 < OWN_BLOCKS, row16, -1) == own_blk
    digits = jnp.concatenate(
        [
            jnp.where(named, (place >> 8).astype(F32), 0.0),
            jnp.where(named, (place & 255).astype(F32), 0.0),
        ],
        axis=0,
    ).astype(BF)
    place_table = dot_nt(digits, onehot_out[...]).astype(BF)

    def renumber(s, carry):
        v = face_slot[pl.ds(s, 1), :]
        col = jnp.broadcast_to(v & 255, (256, ELEM))
        first = (iota((256, ELEM), 0) == col).astype(F32).astype(BF)
        found = dot(place_table, first)
        hit = iota((16, ELEM), 0) == (v >> 8)
        spot = jnp.sum(
            jnp.where(hit, 256.0 * found[0:16] + found[16:32], 0.0), axis=0, keepdims=True
        ).astype(jnp.int32)
        v = jnp.where(spot > 0, OWNED + GHOSTS - 1 + spot, v)
        onehot[s] = (iota((256, ELEM), 0) == (v & 255)).astype(F32).astype(BF)
        blk = (v >> 8).astype(F32)
        blk_f[s] = jnp.broadcast_to(blk, (8, ELEM))
        blk_d[s] = (blk - (iota((48, ELEM), 0) >= 24).astype(F32)).astype(BF)
        idx = 8.0 * blk + material[...].astype(F32)
        idx_f[s] = (idx - iota((16, ELEM), 0).astype(F32)).astype(BF)
        return carry

    lax.fori_loop(0, SIDES, renumber, 0, unroll=True)

    def count(s, carry):
        idx = idx_f[s]
        ones = jnp.concatenate(
            [
                jnp.where(idx == BF(16 * t), BF(1), BF(0))
                for t in range(8 * BLOCKS // 16)
            ],
            axis=0,
        )
        counts[s] = dot_nt(ones, onehot[s])
        return carry

    lax.fori_loop(0, SIDES, count, 0, unroll=True)

    inv_pad[...] = jnp.zeros_like(inv_pad)
    inv_pad[:, 0:NODES, 0:NODES] = inverses[...]
    lift_pad[...] = jnp.zeros_like(lift_pad)
    lift_pad[0:NODES, 0 : SIDES * FNODES] = lift[...]
    src_pad[...] = jnp.zeros_like(src_pad)
    src_pad[0:NODES] = source[...]
    hi, lo = split(src_pad[...])
    src3[0:NP], src3[NP : 2 * NP], src3[2 * NP :] = hi, lo, hi

    side_p, node_p = trace_position(iota((TP, 256), 0))
    order = jnp.where(side_p < SIDES, 6 * node_p + side_p, -1)
    perm = (iota((TP, 256), 1) == order).astype(F32)
    lift_t = dot_nt(perm, lift_pad[...], HIGH)
    lift_p = dot_nt(lift_pad[...], perm, HIGH)
    eye = iota((TP, TP), 0) == iota((TP, TP), 1)
    col = iota((TP, 192), 1)
    for i in range(1, 4):
        col = col - 48 * (iota((TP, 192), 1) >= 48 * i).astype(jnp.int32)
    side_c, _ = trace_position(iota((TP, 192), 0))
    spread = jnp.zeros((TP, 192), F32)
    for m in range(MATS):
        inv = inv_pad[m]
        wm = dot(inv, lift_p, HIGH)
        wt = dot(lift_t, inv, HIGH)
        am = dot(wt, lift_p, HIGH)
        diagonal = jnp.abs(jnp.sum(jnp.where(eye, am, 0.0), axis=1, keepdims=True)) + stab[m]
        spread = spread + jnp.where(col == 8 * side_c + m, diagonal, 0.0)
        am = am + jnp.where(eye, stab[m], 0.0)
        hi, lo = split(am)
        a3[TP * m : TP * (m + 1)] = jnp.concatenate([hi, hi, lo], axis=1)
        hi, lo = split(wm)
        w3[NP * m : NP * (m + 1)] = jnp.concatenate([hi, hi, lo], axis=1)
        hi, lo = split(wt)
        r = slice(TP * m, TP * (m + 1))
        left3[r, 0:NP], left3[r, NP : 2 * NP], left3[r, 2 * NP :] = hi, hi, lo
        hi, lo = split(inv)
        r = slice(MATS * TP + NP * m, MATS * TP + NP * (m + 1))
        left3[r, 0:NP], left3[r, NP : 2 * NP], left3[r, 2 * NP :] = hi, hi, lo
    sdiag = jnp.zeros((24, 192), F32)
    for s in range(SIDES):
        sdiag = sdiag + spread[24 * s : 24 * s + 24]
    last = jnp.sum(spread[144:152], axis=0, keepdims=True)
    sdiag = jnp.concatenate([sdiag, jnp.broadcast_to(last, (8, 192))], axis=0)
    hi = sdiag.astype(BF).astype(F32)
    sdiag = jnp.where(iota((32, 192), 1) < 96, hi, sdiag - hi).astype(BF)

    def diag_block(a):
        _, _, main, left = GROUPS["own" if a < OWN_BLOCKS else "out"]
        b = a if a < OWN_BLOCKS else a - OWN_BLOCKS
        met = jnp.concatenate([counts[s, 8 * a : 8 * a + 8] for s in range(SIDES)], axis=0)
        hi, lo = split(met)
        d = dot(sdiag, jnp.concatenate([hi, lo, hi, lo], axis=0))
        scale[main + 24 * b : main + 24 * b + 24] = d[0:24]
        scale[left + b : left + b + 1] = d[24:25]

    scale[...] = jnp.zeros_like(scale)
    for a in range(OWN_BLOCKS, BLOCKS):
        diag_block(a)
    post(0, scale)

    mat = material[...]

    def pick(y, width, e):
        m_row = jnp.broadcast_to(mat[:, e], (8, y.shape[1]))[None]
        y = y.reshape(MATS, width // 8, 8, y.shape[1])
        return jnp.where(
            m_row == 0, y[0], jnp.where(m_row == 1, y[1], jnp.where(m_row == 2, y[2], y[3]))
        ).reshape(width, y.shape[3])

    CHUNK = 512
    for c in range(ELEM // CHUNK):
        e = slice(c * CHUNK, (c + 1) * CHUNK)
        y = dot(left3[...], src3[:, e])
        rhs_terms[:, e] = pick(y[0 : MATS * TP], TP, e)
        potential[:, e] = pick(y[MATS * TP :], NP, e)[0:NODES]

    def store_terms(terms, e):
        for s in range(SIDES):
            t = terms[24 * s : 24 * s + 24]
            hi, lo = split(jnp.concatenate([t, t], axis=0))
            t_hi[s, :, e], t_lo[s, :, e] = hi, lo
            t = jnp.broadcast_to(terms[144 + s : 145 + s], (16, terms.shape[1]))
            hi, lo = split(t)
            l_hi[s, :, e], l_lo[s, :, e] = hi, lo

    for c in range(ELEM // CHUNK):
        e = slice(c * CHUNK, (c + 1) * CHUNK)
        store_terms(rhs_terms[:, e], e)

    def row_ids(first, last, dtype):
        r = iota((16, ELEM), 0)
        return jnp.where(r < last - first, r + first, -1).astype(F32).astype(dtype)

    def assemble(name):
        first, last, main, left = GROUPS[name]
        rows = slice(main, left + 16)
        partial[rows] = jnp.zeros((left + 16 - main, 256), F32)

        def add(s, carry):
            hit = row_ids(first, last, BF) == blk_d[s, 0:16]
            hits = [blk_d[s] == BF(a) for a in range(first, last, 2)]
            out = None
            for t, l in ((t_hi, l_hi), (t_lo, l_lo)):
                tv = t[s]
                z = jnp.concatenate(
                    [jnp.where(h, tv, BF(0)) for h in hits] + [jnp.where(hit, l[s], BF(0))], axis=0
                )
                d = dot_nt(z, onehot[s])
                out = d if out is None else out + d
            partial[rows] += out
            return carry

        lax.fori_loop(0, SIDES, add, 0, unroll=True)

    def fetch(name):
        first, last, main, left = GROUPS[name]

        def take(s, carry):
            y = dot(table[main : left + 16], onehot[s]) + dot(table2[main : left + 16], onehot[s])
            blk = blk_f[s]
            if name == "own":
                acc = jnp.zeros((3, 8, ELEM), F32)
                acc_left = jnp.zeros((1, ELEM), F32)
            else:
                acc = x_main[s].reshape(3, 8, ELEM)
                acc_left = x_left[s, 0:1]
            for a in range(first, last):
                ya = y[24 * (a - first) : 24 * (a - first) + 24].reshape(3, 8, ELEM)
                acc = jnp.where((blk == F32(a))[None], ya, acc)
            x_main[s] = acc.reshape(24, ELEM)
            hit = row_ids(first, last, F32).reshape(2, 8, ELEM) == blk[None]
            yl = jnp.where(hit, y[left - main :].reshape(2, 8, ELEM), 0.0)
            x_left[s, 0:1] = acc_left + jnp.sum(yl[0] + yl[1], axis=0, keepdims=True)
            return carry

        lax.fori_loop(0, SIDES, take, 0, unroll=True)

    def gathered():
        rows = [x_main[s] for s in range(SIDES)]
        x = jnp.concatenate([x_left[s, 0:1] for s in range(SIDES)] + [jnp.zeros((10, ELEM), F32)], axis=0)
        x = jnp.concatenate(rows + [x], axis=0)
        hi, lo = split(x)
        x3[0:TP], x3[TP : 2 * TP], x3[2 * TP :] = hi, lo, hi

    def table_rows(name):
        _, _, main, left = GROUPS[name]
        return slice(main, left + 16)

    def update(name, first):
        rows = table_rows(name)
        step = scale[rows] * partial[rows]
        x = step if first else total[rows] + step
        total[rows] = x
        hi, lo = split(x)
        table[rows], table2[rows] = hi, lo

    assemble("out")
    post(1, partial)
    for a in range(OWN_BLOCKS):
        diag_block(a)
    assemble("own")

    def invert(name):
        rows = table_rows(name)
        d = scale[rows]
        scale[rows] = jnp.where(d == 0.0, 0.0, DAMPING / jnp.where(d == 0.0, 1.0, d))

    invert("own")
    update("own", True)
    fetch("own")
    collect(0, scale)
    collect(1, partial)
    invert("out")
    update("out", True)
    fetch("out")

    for sweep in range(SWEEPS - 1):
        gathered()
        for c in range(ELEM // CHUNK):
            e = slice(c * CHUNK, (c + 1) * CHUNK)
            y = pick(dot(a3[...], x3[:, e]), TP, e)
            store_terms(rhs_terms[:, e] - y, e)
        assemble("out")
        post(2 + sweep, partial)
        assemble("own")
        update("own", False)
        fetch("own")
        collect(2 + sweep, partial)
        update("out", False)
        fetch("out")

    rows = slice(OWN_MAIN, OWN_LEFT + 16)
    back = jnp.zeros((304, 256), F32)
    for b in range(3):
        cols = slice(256 * b, 256 * (b + 1))
        r = OUT_MAIN + 24 * (b + 3)
        x = total[r : r + 24]
        xl = jnp.broadcast_to(total[OUT_LEFT + b + 3 : OUT_LEFT + b + 4], (16, 256))
        blk = own_blk[:, cols].astype(F32)
        blk2 = (blk - (iota((48, 256), 0) >= 24).astype(F32)).astype(BF)
        hits = [blk2 == BF(a) for a in range(0, OWN_BLOCKS, 2)]
        r16 = iota((16, 256), 0)
        hit = jnp.where(r16 < OWN_BLOCKS, r16, -1).astype(F32).astype(BF) == blk.astype(BF)
        for xv, lv in zip(split(jnp.concatenate([x, x], axis=0)), split(xl)):
            z = jnp.concatenate(
                [jnp.where(h, xv, BF(0)) for h in hits] + [jnp.where(hit, lv, BF(0))], axis=0
            )
            back = back + dot_nt(z, onehot_out[:, cols])
    full = total[rows] + back
    for a in range(OWN_BLOCKS):
        cols = slice(256 * a, 256 * (a + 1))
        trace_own[0:24, cols] = full[24 * a : 24 * a + 24]
        trace_own[24:25, cols] = full[OWN_LEFT + a : OWN_LEFT + a + 1]

    gathered()
    for c in range(ELEM // CHUNK):
        e = slice(c * CHUNK, (c + 1) * CHUNK)
        y = pick(dot(w3[...], x3[:, e]), NP, e)
        potential[:, e] = potential[:, e] - y[0:NODES]

    for r in range(ROUNDS):
        for k in range(4):
            @pl.when(there[k])
            def _():
                copy(r, k).wait_send()


def shards(source, inverses, lift, stab, material, face_slot, owner_map):
    vmem = pl.BlockSpec(memory_space=pltpu.VMEM)
    smem = pl.BlockSpec(memory_space=pltpu.SMEM)
    v = pltpu.VMEM
    return pl.pallas_call(
        kernel,
        out_shape=(
            jax.ShapeDtypeStruct((NODES, ELEM), F32),
            jax.ShapeDtypeStruct((FNODES, OWNED), F32),
        ),
        in_specs=[vmem, vmem, vmem, smem, vmem, vmem, vmem],
        out_specs=(vmem, vmem),
        scratch_shapes=[
            v((SIDES, 256, ELEM), BF),
            v((256, GHOSTS), BF),
            v((SIDES, 8, ELEM), F32),
            v((SIDES, 48, ELEM), BF),
            v((SIDES, 16, ELEM), BF),
            v((SIDES, 8 * BLOCKS, 256), F32),
            v((MATS, NP, NP), F32),
            v((NP, 256), F32),
            v((NP, ELEM), F32),
            v((3 * NP, ELEM), BF),
            v((MATS * (TP + NP), 3 * NP), BF),
            v((MATS * TP, 3 * TP), BF),
            v((MATS * NP, 3 * TP), BF),
            v((TP, ELEM), F32),
            v((SIDES, 24, ELEM), F32),
            v((SIDES, 8, ELEM), F32),
            v((3 * TP, ELEM), BF),
            v((SIDES, 48, ELEM), BF),
            v((SIDES, 48, ELEM), BF),
            v((SIDES, 16, ELEM), BF),
            v((SIDES, 16, ELEM), BF),
            v((ROWS, 256), F32),
            v((ROWS, 256), F32),
            v((ROWS, 256), BF),
            v((ROWS, 256), BF),
            v((ROWS, 256), F32),
            v((ROUNDS, 2, SENT, CAP_W), F32),
            v((ROUNDS, 2, SENT, CAP_W), F32),
            v((ROUNDS, 2, SENT, CAP_N), F32),
            v((ROUNDS, 2, SENT, CAP_N), F32),
            pltpu.SemaphoreType.DMA((ROUNDS, 4)),
            pltpu.SemaphoreType.DMA((ROUNDS, 4)),
        ],
        compiler_params=pltpu.CompilerParams(
            collective_id=0, has_side_effects=True, vmem_limit_bytes=48 * 2**20
        ),
    )(source, inverses, lift, stab, material.reshape(1, ELEM), face_slot, owner_map)


def solution(mesh):
    both = ("wide", "narrow")
    return jax.shard_map(
        shards,
        mesh=mesh,
        in_specs=(
            P(None, both), P(), P(), P(), P(both), P(None, both), P(both, None),
        ),
        out_specs=(P(None, both), P(None, both)),
        check_vma=False,
    )
```

```python
import functools

import jax
import jax.numpy as jnp
from jax import lax
from jax.experimental import pallas as pl
from jax.experimental.pallas import tpu as pltpu
from jax.sharding import PartitionSpec as P

MESH = pl.DeviceIdType.MESH
F32, BF = jnp.float32, jnp.bfloat16
HIGH = lax.Precision.HIGHEST
DAMPING = 0.6
SWEEPS = 3

NODES, FNODES, SIDES, MATS = 125, 25, 6, 4
ELEM = 1024
OWNED = 3 * ELEM
CAP_W, CAP_N = 256, 128
GHOSTS = 2 * CAP_W + 2 * CAP_N
TP = 160
NP = 128

OWN_BLOCKS, BLOCKS = 12, 18
OWN_MAIN, OWN_LEFT, OUT_MAIN, OUT_LEFT, ROWS = 0, 288, 304, 448, 464
GROUPS = {
    "own": (0, 12, OWN_MAIN, OWN_LEFT),
    "out": (12, 18, OUT_MAIN, OUT_LEFT),
}
SENT = 56
ROUNDS = 2 + SWEEPS - 1


def dot(a, b, precision=None):
    return jnp.dot(a, b, precision=precision, preferred_element_type=F32)


def dot_nt(a, b, precision=None):
    return lax.dot_general(
        a, b, (((1,), (1,)), ((), ())), precision=precision, preferred_element_type=F32
    )


def split(x):
    hi = x.astype(BF)
    return hi, (x - hi.astype(F32)).astype(BF)


def iota(shape, dim):
    return lax.broadcasted_iota(jnp.int32, shape, dim)


def trace_position(p):
    side = jnp.zeros_like(p)
    for i in range(1, SIDES):
        side = side + (p >= 24 * i).astype(jnp.int32)
    node = jnp.where(p < 144, p - 24 * side, 24)
    side = jnp.where(p < 144, side, p - 144)
    return side, node


def kernel(
    source, inverses, lift, stab, material, face_slot, owner_map,
    potential, trace_own,
    onehot, onehot_out, blk_f, blk_d, idx_f, counts,
    inv_pad, lift_pad, src_pad, src3, left3, a3, w3,
    rhs_terms, x_main, x_left, x3, t_hi, t_lo, l_hi, l_lo,
    partial, total, table, table2, scale,
    send_w, recv_w, send_n, recv_n, send_sems, recv_sems,
):
    w, n = lax.axis_index("wide"), lax.axis_index("narrow")
    wide, narrow = lax.axis_size("wide"), lax.axis_size("narrow")
    neighbour = (
        (lax.rem(w + wide - 1, wide), n),
        (lax.rem(w + 1, wide), n),
        (w, lax.rem(n + narrow - 1, narrow)),
        (w, lax.rem(n + 1, narrow)),
    )
    barrier = pltpu.get_barrier_semaphore()
    for k in range(4):
        pl.semaphore_signal(barrier, inc=1, device_id=neighbour[k], device_id_type=MESH)
    pl.semaphore_wait(barrier, 4)

    def buffers(k):
        return (send_w, recv_w, k) if k < 2 else (send_n, recv_n, k - 2)

    def copy(r, k):
        send, recv, side = buffers(k)
        return pltpu.make_async_remote_copy(
            src_ref=send.at[r, side],
            dst_ref=recv.at[r, 1 - side],
            send_sem=send_sems.at[r, k],
            recv_sem=recv_sems.at[r, k ^ 1],
            device_id=neighbour[k],
            device_id_type=MESH,
        )

    def arrival(r, k):
        send, recv, side = buffers(k)
        return pltpu.make_async_remote_copy(
            src_ref=send.at[r, side],
            dst_ref=recv.at[r, side],
            send_sem=send_sems.at[r, k],
            recv_sem=recv_sems.at[r, k],
            device_id=neighbour[k],
            device_id_type=MESH,
        )

    def places(k):
        block = min(k, 2)
        lo, width = (0, CAP_W) if k < 2 else ((k - 2) * CAP_N, CAP_N)
        return block, slice(lo, lo + width)

    def post(r, values):
        for k in range(4):
            send, recv, side = buffers(k)
            block, cols = places(k)
            ghost, shared = OUT_MAIN + 24 * block, OUT_MAIN + 24 * (block + 3)
            send[r, side, 0:24] = values[ghost : ghost + 24, cols]
            send[r, side, 24:48] = values[shared : shared + 24, cols]
            ghost, shared = OUT_LEFT + block, OUT_LEFT + block + 3
            send[r, side, 48:49] = values[ghost : ghost + 1, cols]
            send[r, side, 49:50] = values[shared : shared + 1, cols]

            copy(r, k).start()

    def collect(r, values):
        for k in range(4):
            arrival(r, k).wait_recv()

        for k in range(4):
            send, recv, side = buffers(k)
            block, cols = places(k)
            ghost, shared = OUT_MAIN + 24 * block, OUT_MAIN + 24 * (block + 3)
            values[shared : shared + 24, cols] += recv[r, side, 0:24]
            values[ghost : ghost + 24, cols] += recv[r, side, 24:48]
            ghost, shared = OUT_LEFT + block, OUT_LEFT + block + 3
            values[shared : shared + 1, cols] += recv[r, side, 48:49]
            values[ghost : ghost + 1, cols] += recv[r, side, 49:50]

    owners = owner_map[...]
    own_blk, own_col = owners >> 8, owners & 255
    place = iota((1, GHOSTS), 1) + 1
    onehot_out[...] = (iota((256, GHOSTS), 0) == own_col).astype(F32).astype(BF)
    row16 = iota((16, GHOSTS), 0)
    named = jnp.where(row16 < OWN_BLOCKS, row16, -1) == own_blk
    digits = jnp.concatenate(
        [
            jnp.where(named, (place >> 8).astype(F32), 0.0),
            jnp.where(named, (place & 255).astype(F32), 0.0),
        ],
        axis=0,
    ).astype(BF)
    place_table = dot_nt(digits, onehot_out[...]).astype(BF)

    def renumber(s, carry):
        v = face_slot[pl.ds(s, 1), :]
        col = jnp.broadcast_to(v & 255, (256, ELEM))
        first = (iota((256, ELEM), 0) == col).astype(F32).astype(BF)
        found = dot(place_table, first)
        hit = iota((16, ELEM), 0) == (v >> 8)
        spot = jnp.sum(
            jnp.where(hit, 256.0 * found[0:16] + found[16:32], 0.0), axis=0, keepdims=True
        ).astype(jnp.int32)
        v = jnp.where(spot > 0, OWNED + GHOSTS - 1 + spot, v)
        onehot[s] = (iota((256, ELEM), 0) == (v & 255)).astype(F32).astype(BF)
        blk = (v >> 8).astype(F32)
        blk_f[s] = jnp.broadcast_to(blk, (8, ELEM))
        blk_d[s] = (blk - (iota((48, ELEM), 0) >= 24).astype(F32)).astype(BF)
        idx = 8.0 * blk + material[...].astype(F32)
        idx_f[s] = (idx - iota((16, ELEM), 0).astype(F32)).astype(BF)
        return carry

    lax.fori_loop(0, SIDES, renumber, 0, unroll=True)

    def count(s, carry):
        idx = idx_f[s]
        ones = jnp.concatenate(
            [
                jnp.where(idx == BF(16 * t), BF(1), BF(0))
                for t in range(8 * BLOCKS // 16)
            ],
            axis=0,
        )
        counts[s] = dot_nt(ones, onehot[s])
        return carry

    lax.fori_loop(0, SIDES, count, 0, unroll=True)

    inv_pad[...] = jnp.zeros_like(inv_pad)
    inv_pad[:, 0:NODES, 0:NODES] = inverses[...]
    lift_pad[...] = jnp.zeros_like(lift_pad)
    lift_pad[0:NODES, 0 : SIDES * FNODES] = lift[...]
    src_pad[...] = jnp.zeros_like(src_pad)
    src_pad[0:NODES] = source[...]
    hi, lo = split(src_pad[...])
    src3[0:NP], src3[NP : 2 * NP], src3[2 * NP :] = hi, lo, hi

    side_p, node_p = trace_position(iota((TP, 256), 0))
    order = jnp.where(side_p < SIDES, 6 * node_p + side_p, -1)
    perm = (iota((TP, 256), 1) == order).astype(F32)
    lift_t = dot_nt(perm, lift_pad[...], HIGH)
    lift_p = dot_nt(lift_pad[...], perm, HIGH)
    eye = iota((TP, TP), 0) == iota((TP, TP), 1)
    col = iota((TP, 192), 1)
    for i in range(1, 4):
        col = col - 48 * (iota((TP, 192), 1) >= 48 * i).astype(jnp.int32)
    side_c, _ = trace_position(iota((TP, 192), 0))
    spread = jnp.zeros((TP, 192), F32)
    for m in range(MATS):
        inv = inv_pad[m]
        wm = dot(inv, lift_p, HIGH)
        wt = dot(lift_t, inv, HIGH)
        am = dot(wt, lift_p, HIGH)
        diagonal = jnp.abs(jnp.sum(jnp.where(eye, am, 0.0), axis=1, keepdims=True)) + stab[m]
        spread = spread + jnp.where(col == 8 * side_c + m, diagonal, 0.0)
        am = am + jnp.where(eye, stab[m], 0.0)
        hi, lo = split(am)
        a3[TP * m : TP * (m + 1)] = jnp.concatenate([hi, hi, lo], axis=1)
        hi, lo = split(wm)
        w3[NP * m : NP * (m + 1)] = jnp.concatenate([hi, hi, lo], axis=1)
        hi, lo = split(wt)
        r = slice(TP * m, TP * (m + 1))
        left3[r, 0:NP], left3[r, NP : 2 * NP], left3[r, 2 * NP :] = hi, hi, lo
        hi, lo = split(inv)
        r = slice(MATS * TP + NP * m, MATS * TP + NP * (m + 1))
        left3[r, 0:NP], left3[r, NP : 2 * NP], left3[r, 2 * NP :] = hi, hi, lo
    sdiag = jnp.zeros((24, 192), F32)
    for s in range(SIDES):
        sdiag = sdiag + spread[24 * s : 24 * s + 24]
    last = jnp.sum(spread[144:152], axis=0, keepdims=True)
    sdiag = jnp.concatenate([sdiag, jnp.broadcast_to(last, (8, 192))], axis=0)
    hi = sdiag.astype(BF).astype(F32)
    sdiag = jnp.where(iota((32, 192), 1) < 96, hi, sdiag - hi).astype(BF)

    def diag_block(a):
        _, _, main, left = GROUPS["own" if a < OWN_BLOCKS else "out"]
        b = a if a < OWN_BLOCKS else a - OWN_BLOCKS
        met = jnp.concatenate([counts[s, 8 * a : 8 * a + 8] for s in range(SIDES)], axis=0)
        hi, lo = split(met)
        d = dot(sdiag, jnp.concatenate([hi, lo, hi, lo], axis=0))
        scale[main + 24 * b : main + 24 * b + 24] = d[0:24]
        scale[left + b : left + b + 1] = d[24:25]

    scale[...] = jnp.zeros_like(scale)
    for a in range(OWN_BLOCKS, BLOCKS):
        diag_block(a)
    post(0, scale)

    mat = material[...]

    def pick(y, width, e):
        m_row = jnp.broadcast_to(mat[:, e], (8, y.shape[1]))[None]
        y = y.reshape(MATS, width // 8, 8, y.shape[1])
        return jnp.where(
            m_row == 0, y[0], jnp.where(m_row == 1, y[1], jnp.where(m_row == 2, y[2], y[3]))
        ).reshape(width, y.shape[3])

    CHUNK = 512
    for c in range(ELEM // CHUNK):
        e = slice(c * CHUNK, (c + 1) * CHUNK)
        y = dot(left3[...], src3[:, e])
        rhs_terms[:, e] = pick(y[0 : MATS * TP], TP, e)
        potential[:, e] = pick(y[MATS * TP :], NP, e)[0:NODES]

    def store_terms(terms, e):
        for s in range(SIDES):
            t = terms[24 * s : 24 * s + 24]
            hi, lo = split(jnp.concatenate([t, t], axis=0))
            t_hi[s, :, e], t_lo[s, :, e] = hi, lo
            t = jnp.broadcast_to(terms[144 + s : 145 + s], (16, terms.shape[1]))
            hi, lo = split(t)
            l_hi[s, :, e], l_lo[s, :, e] = hi, lo

    for c in range(ELEM // CHUNK):
        e = slice(c * CHUNK, (c + 1) * CHUNK)
        store_terms(rhs_terms[:, e], e)

    def row_ids(first, last, dtype):
        r = iota((16, ELEM), 0)
        return jnp.where(r < last - first, r + first, -1).astype(F32).astype(dtype)

    def assemble(name):
        first, last, main, left = GROUPS[name]
        rows = slice(main, left + 16)
        partial[rows] = jnp.zeros((left + 16 - main, 256), F32)

        def add(s, carry):
            hit = row_ids(first, last, BF) == blk_d[s, 0:16]
            hits = [blk_d[s] == BF(a) for a in range(first, last, 2)]
            out = None
            for t, l in ((t_hi, l_hi), (t_lo, l_lo)):
                tv = t[s]
                z = jnp.concatenate(
                    [jnp.where(h, tv, BF(0)) for h in hits] + [jnp.where(hit, l[s], BF(0))], axis=0
                )
                d = dot_nt(z, onehot[s])
                out = d if out is None else out + d
            partial[rows] += out
            return carry

        lax.fori_loop(0, SIDES, add, 0, unroll=True)

    def fetch(name):
        first, last, main, left = GROUPS[name]

        def take(s, carry):
            y = dot(table[main : left + 16], onehot[s]) + dot(table2[main : left + 16], onehot[s])
            blk = blk_f[s]
            if name == "own":
                acc = jnp.zeros((3, 8, ELEM), F32)
                acc_left = jnp.zeros((1, ELEM), F32)
            else:
                acc = x_main[s].reshape(3, 8, ELEM)
                acc_left = x_left[s, 0:1]
            for a in range(first, last):
                ya = y[24 * (a - first) : 24 * (a - first) + 24].reshape(3, 8, ELEM)
                acc = jnp.where((blk == F32(a))[None], ya, acc)
            x_main[s] = acc.reshape(24, ELEM)
            hit = row_ids(first, last, F32).reshape(2, 8, ELEM) == blk[None]
            yl = jnp.where(hit, y[left - main :].reshape(2, 8, ELEM), 0.0)
            x_left[s, 0:1] = acc_left + jnp.sum(yl[0] + yl[1], axis=0, keepdims=True)
            return carry

        lax.fori_loop(0, SIDES, take, 0, unroll=True)

    def gathered():
        rows = [x_main[s] for s in range(SIDES)]
        x = jnp.concatenate([x_left[s, 0:1] for s in range(SIDES)] + [jnp.zeros((10, ELEM), F32)], axis=0)
        x = jnp.concatenate(rows + [x], axis=0)
        hi, lo = split(x)
        x3[0:TP], x3[TP : 2 * TP], x3[2 * TP :] = hi, lo, hi

    def table_rows(name):
        _, _, main, left = GROUPS[name]
        return slice(main, left + 16)

    def update(name, first):
        rows = table_rows(name)
        step = scale[rows] * partial[rows]
        x = step if first else total[rows] + step
        total[rows] = x
        hi, lo = split(x)
        table[rows], table2[rows] = hi, lo

    assemble("out")
    post(1, partial)
    for a in range(OWN_BLOCKS):
        diag_block(a)
    assemble("own")

    def invert(name):
        rows = table_rows(name)
        d = scale[rows]
        scale[rows] = jnp.where(d == 0.0, 0.0, DAMPING / jnp.where(d == 0.0, 1.0, d))

    invert("own")
    update("own", True)
    fetch("own")
    collect(0, scale)
    collect(1, partial)
    invert("out")
    update("out", True)
    fetch("out")

    for sweep in range(SWEEPS - 1):
        gathered()
        for c in range(ELEM // CHUNK):
            e = slice(c * CHUNK, (c + 1) * CHUNK)
            y = pick(dot(a3[...], x3[:, e]), TP, e)
            store_terms(rhs_terms[:, e] - y, e)
        assemble("out")
        post(2 + sweep, partial)
        assemble("own")
        update("own", False)
        fetch("own")
        collect(2 + sweep, partial)
        update("out", False)
        fetch("out")

    rows = slice(OWN_MAIN, OWN_LEFT + 16)
    back = jnp.zeros((304, 256), F32)
    for b in range(3):
        cols = slice(256 * b, 256 * (b + 1))
        r = OUT_MAIN + 24 * (b + 3)
        x = total[r : r + 24]
        xl = jnp.broadcast_to(total[OUT_LEFT + b + 3 : OUT_LEFT + b + 4], (16, 256))
        blk = own_blk[:, cols].astype(F32)
        blk2 = (blk - (iota((48, 256), 0) >= 24).astype(F32)).astype(BF)
        hits = [blk2 == BF(a) for a in range(0, OWN_BLOCKS, 2)]
        r16 = iota((16, 256), 0)
        hit = jnp.where(r16 < OWN_BLOCKS, r16, -1).astype(F32).astype(BF) == blk.astype(BF)
        for xv, lv in zip(split(jnp.concatenate([x, x], axis=0)), split(xl)):
            z = jnp.concatenate(
                [jnp.where(h, xv, BF(0)) for h in hits] + [jnp.where(hit, lv, BF(0))], axis=0
            )
            back = back + dot_nt(z, onehot_out[:, cols])
    full = total[rows] + back
    for a in range(OWN_BLOCKS):
        cols = slice(256 * a, 256 * (a + 1))
        trace_own[0:24, cols] = full[24 * a : 24 * a + 24]
        trace_own[24:25, cols] = full[OWN_LEFT + a : OWN_LEFT + a + 1]

    gathered()
    for c in range(ELEM // CHUNK):
        e = slice(c * CHUNK, (c + 1) * CHUNK)
        y = pick(dot(w3[...], x3[:, e]), NP, e)
        potential[:, e] = potential[:, e] - y[0:NODES]

    for r in range(ROUNDS):
        for k in range(4):
            copy(r, k).wait_send()


def shards(source, inverses, lift, stab, material, face_slot, owner_map):
    vmem = pl.BlockSpec(memory_space=pltpu.VMEM)
    smem = pl.BlockSpec(memory_space=pltpu.SMEM)
    v = pltpu.VMEM
    return pl.pallas_call(
        kernel,
        out_shape=(
            jax.ShapeDtypeStruct((NODES, ELEM), F32),
            jax.ShapeDtypeStruct((FNODES, OWNED), F32),
        ),
        in_specs=[vmem, vmem, vmem, smem, vmem, vmem, vmem],
        out_specs=(vmem, vmem),
        scratch_shapes=[
            v((SIDES, 256, ELEM), BF),
            v((256, GHOSTS), BF),
            v((SIDES, 8, ELEM), F32),
            v((SIDES, 48, ELEM), BF),
            v((SIDES, 16, ELEM), BF),
            v((SIDES, 8 * BLOCKS, 256), F32),
            v((MATS, NP, NP), F32),
            v((NP, 256), F32),
            v((NP, ELEM), F32),
            v((3 * NP, ELEM), BF),
            v((MATS * (TP + NP), 3 * NP), BF),
            v((MATS * TP, 3 * TP), BF),
            v((MATS * NP, 3 * TP), BF),
            v((TP, ELEM), F32),
            v((SIDES, 24, ELEM), F32),
            v((SIDES, 8, ELEM), F32),
            v((3 * TP, ELEM), BF),
            v((SIDES, 48, ELEM), BF),
            v((SIDES, 48, ELEM), BF),
            v((SIDES, 16, ELEM), BF),
            v((SIDES, 16, ELEM), BF),
            v((ROWS, 256), F32),
            v((ROWS, 256), F32),
            v((ROWS, 256), BF),
            v((ROWS, 256), BF),
            v((ROWS, 256), F32),
            v((ROUNDS, 2, SENT, CAP_W), F32),
            v((ROUNDS, 2, SENT, CAP_W), F32),
            v((ROUNDS, 2, SENT, CAP_N), F32),
            v((ROUNDS, 2, SENT, CAP_N), F32),
            pltpu.SemaphoreType.DMA((ROUNDS, 4)),
            pltpu.SemaphoreType.DMA((ROUNDS, 4)),
        ],
        compiler_params=pltpu.CompilerParams(
            collective_id=0, has_side_effects=True, vmem_limit_bytes=48 * 2**20
        ),
    )(source, inverses, lift, stab, material.reshape(1, ELEM), face_slot, owner_map)


def solution(mesh):
    both = ("wide", "narrow")
    return jax.shard_map(
        shards,
        mesh=mesh,
        in_specs=(
            P(None, both), P(), P(), P(), P(both), P(None, both), P(both, None),
        ),
        out_specs=(P(None, both), P(None, both)),
        check_vma=False,
    )
```

```python
import functools

import jax
import jax.numpy as jnp
from jax import lax
from jax.experimental import pallas as pl
from jax.experimental.pallas import tpu as pltpu
from jax.sharding import PartitionSpec as P

MESH = pl.DeviceIdType.MESH
F32, BF = jnp.float32, jnp.bfloat16
HIGH = lax.Precision.HIGHEST
DAMPING = 0.6
SWEEPS = 3

NODES, FNODES, SIDES, MATS = 125, 25, 6, 4
ELEM = 1024
OWNED = 3 * ELEM
CAP_W, CAP_N = 256, 128
GHOSTS = 2 * CAP_W + 2 * CAP_N
TP = 160
NP = 128

OWN_BLOCKS, BLOCKS = 12, 18
OWN_MAIN, OWN_LEFT, OUT_MAIN, OUT_LEFT, ROWS = 0, 288, 304, 448, 464
GROUPS = {
    "own": (0, 12, OWN_MAIN, OWN_LEFT),
    "out": (12, 18, OUT_MAIN, OUT_LEFT),
}
SENT = 56
ROUNDS = 2 + SWEEPS - 1


def dot(a, b, precision=None):
    return jnp.dot(a, b, precision=precision, preferred_element_type=F32)


def dot_nt(a, b, precision=None):
    return lax.dot_general(
        a, b, (((1,), (1,)), ((), ())), precision=precision, preferred_element_type=F32
    )


def split(x):
    hi = x.astype(BF)
    return hi, (x - hi.astype(F32)).astype(BF)


def iota(shape, dim):
    return lax.broadcasted_iota(jnp.int32, shape, dim)


def trace_position(p):
    side = jnp.zeros_like(p)
    for i in range(1, SIDES):
        side = side + (p >= 24 * i).astype(jnp.int32)
    node = jnp.where(p < 144, p - 24 * side, 24)
    side = jnp.where(p < 144, side, p - 144)
    return side, node


def kernel(
    source, inverses, lift, stab, material, face_slot, owner_map,
    potential, trace_own,
    onehot, onehot_out, blk_f, blk_d, idx_f, counts,
    inv_pad, lift_pad, src_pad, src3, left3, a3, w3,
    rhs_terms, x_main, x_left, x3, t_hi, t_lo, l_hi, l_lo,
    partial, total, table, table2, scale,
    send_w, recv_w, send_n, recv_n, send_sems, recv_sems,
):
    w, n = lax.axis_index("wide"), lax.axis_index("narrow")
    wide, narrow = lax.axis_size("wide"), lax.axis_size("narrow")
    ends = (w == 0, w == wide - 1, n == 0, n == narrow - 1)
    one = (w ^ 1, n ^ 1)
    neighbour = (
        (jnp.where(ends[0], w, w - 1), jnp.where(ends[0], one[1], n)),
        (jnp.where(ends[1], w, w + 1), jnp.where(ends[1], one[1], n)),
        (jnp.where(ends[2], one[0], w), jnp.where(ends[2], n, n - 1)),
        (jnp.where(ends[3], one[0], w), jnp.where(ends[3], n, n + 1)),
    )
    barrier = pltpu.get_barrier_semaphore()
    for k in range(4):
        pl.semaphore_signal(barrier, inc=1, device_id=neighbour[k], device_id_type=MESH)
    pl.semaphore_wait(barrier, 4)

    def buffers(k):
        return (send_w, recv_w, k) if k < 2 else (send_n, recv_n, k - 2)

    def copy(r, k):
        send, recv, side = buffers(k)
        return pltpu.make_async_remote_copy(
            src_ref=send.at[r, side],
            dst_ref=recv.at[r, jnp.where(ends[k], side, 1 - side)],
            send_sem=send_sems.at[r, k],
            recv_sem=recv_sems.at[r, jnp.where(ends[k], k, k ^ 1)],
            device_id=neighbour[k],
            device_id_type=MESH,
        )

    def arrival(r, k):
        send, recv, side = buffers(k)
        return pltpu.make_async_remote_copy(
            src_ref=send.at[r, side],
            dst_ref=recv.at[r, side],
            send_sem=send_sems.at[r, k],
            recv_sem=recv_sems.at[r, k],
            device_id=neighbour[k],
            device_id_type=MESH,
        )

    def places(k):
        block = min(k, 2)
        lo, width = (0, CAP_W) if k < 2 else ((k - 2) * CAP_N, CAP_N)
        return block, slice(lo, lo + width)

    def post(r, values):
        for k in range(4):
            send, recv, side = buffers(k)
            block, cols = places(k)
            ghost, shared = OUT_MAIN + 24 * block, OUT_MAIN + 24 * (block + 3)
            send[r, side, 0:24] = values[ghost : ghost + 24, cols]
            send[r, side, 24:48] = values[shared : shared + 24, cols]
            ghost, shared = OUT_LEFT + block, OUT_LEFT + block + 3
            send[r, side, 48:49] = values[ghost : ghost + 1, cols]
            send[r, side, 49:50] = values[shared : shared + 1, cols]

            copy(r, k).start()

    def collect(r, values):
        for k in range(4):
            arrival(r, k).wait_recv()

        for k in range(4):
            send, recv, side = buffers(k)
            block, cols = places(k)
            ghost, shared = OUT_MAIN + 24 * block, OUT_MAIN + 24 * (block + 3)
            values[shared : shared + 24, cols] += recv[r, side, 0:24]
            values[ghost : ghost + 24, cols] += recv[r, side, 24:48]
            ghost, shared = OUT_LEFT + block, OUT_LEFT + block + 3
            values[shared : shared + 1, cols] += recv[r, side, 48:49]
            values[ghost : ghost + 1, cols] += recv[r, side, 49:50]

    owners = owner_map[...]
    own_blk, own_col = owners >> 8, owners & 255
    place = iota((1, GHOSTS), 1) + 1
    onehot_out[...] = (iota((256, GHOSTS), 0) == own_col).astype(F32).astype(BF)
    row16 = iota((16, GHOSTS), 0)
    named = jnp.where(row16 < OWN_BLOCKS, row16, -1) == own_blk
    digits = jnp.concatenate(
        [
            jnp.where(named, (place >> 8).astype(F32), 0.0),
            jnp.where(named, (place & 255).astype(F32), 0.0),
        ],
        axis=0,
    ).astype(BF)
    place_table = dot_nt(digits, onehot_out[...]).astype(BF)

    def renumber(s, carry):
        v = face_slot[pl.ds(s, 1), :]
        col = jnp.broadcast_to(v & 255, (256, ELEM))
        first = (iota((256, ELEM), 0) == col).astype(F32).astype(BF)
        found = dot(place_table, first)
        hit = iota((16, ELEM), 0) == (v >> 8)
        spot = jnp.sum(
            jnp.where(hit, 256.0 * found[0:16] + found[16:32], 0.0), axis=0, keepdims=True
        ).astype(jnp.int32)
        v = jnp.where(spot > 0, OWNED + GHOSTS - 1 + spot, v)
        onehot[s] = (iota((256, ELEM), 0) == (v & 255)).astype(F32).astype(BF)
        blk = (v >> 8).astype(F32)
        blk_f[s] = jnp.broadcast_to(blk, (8, ELEM))
        blk_d[s] = (blk - (iota((48, ELEM), 0) >= 24).astype(F32)).astype(BF)
        idx = 8.0 * blk + material[...].astype(F32)
        idx_f[s] = (idx - iota((16, ELEM), 0).astype(F32)).astype(BF)
        return carry

    lax.fori_loop(0, SIDES, renumber, 0, unroll=True)

    def count(s, carry):
        idx = idx_f[s]
        ones = jnp.concatenate(
            [
                jnp.where(idx == BF(16 * t), BF(1), BF(0))
                for t in range(8 * BLOCKS // 16)
            ],
            axis=0,
        )
        counts[s] = dot_nt(ones, onehot[s])
        return carry

    lax.fori_loop(0, SIDES, count, 0, unroll=True)

    inv_pad[...] = jnp.zeros_like(inv_pad)
    for m in range(MATS):
        inv_pad[m, 0:NODES, 0:NODES] = inverses[:, m, :]
    lift_pad[...] = jnp.zeros_like(lift_pad)
    lift_pad[0 : SIDES * FNODES, 0:NODES] = lift[...]
    src_pad[...] = jnp.zeros_like(src_pad)
    src_pad[0:NODES] = source[...]
    hi, lo = split(src_pad[...])
    src3[0:NP], src3[NP : 2 * NP], src3[2 * NP :] = hi, lo, hi

    side_p, node_p = trace_position(iota((TP, 256), 0))
    order = jnp.where(side_p < SIDES, 6 * node_p + side_p, -1)
    perm = (iota((TP, 256), 1) == order).astype(F32)
    lift_t = dot(perm, lift_pad[...], HIGH)
    eye = iota((TP, TP), 0) == iota((TP, TP), 1)
    col = iota((TP, 192), 1)
    for i in range(1, 4):
        col = col - 48 * (iota((TP, 192), 1) >= 48 * i).astype(jnp.int32)
    side_c, _ = trace_position(iota((TP, 192), 0))
    spread = jnp.zeros((TP, 192), F32)
    for m in range(MATS):
        inv = inv_pad[m]
        wm = dot_nt(inv, lift_t, HIGH)
        wt = dot(lift_t, inv, HIGH)
        am = dot_nt(wt, lift_t, HIGH)
        diagonal = jnp.abs(jnp.sum(jnp.where(eye, am, 0.0), axis=1, keepdims=True)) + stab[m]
        spread = spread + jnp.where(col == 8 * side_c + m, diagonal, 0.0)
        am = am + jnp.where(eye, stab[m], 0.0)
        hi, lo = split(am)
        a3[TP * m : TP * (m + 1)] = jnp.concatenate([hi, hi, lo], axis=1)
        hi, lo = split(wm)
        w3[NP * m : NP * (m + 1)] = jnp.concatenate([hi, hi, lo], axis=1)
        hi, lo = split(wt)
        r = slice(TP * m, TP * (m + 1))
        left3[r, 0:NP], left3[r, NP : 2 * NP], left3[r, 2 * NP :] = hi, hi, lo
        hi, lo = split(inv)
        r = slice(MATS * TP + NP * m, MATS * TP + NP * (m + 1))
        left3[r, 0:NP], left3[r, NP : 2 * NP], left3[r, 2 * NP :] = hi, hi, lo
    sdiag = jnp.zeros((24, 192), F32)
    for s in range(SIDES):
        sdiag = sdiag + spread[24 * s : 24 * s + 24]
    last = jnp.sum(spread[144:152], axis=0, keepdims=True)
    sdiag = jnp.concatenate([sdiag, jnp.broadcast_to(last, (8, 192))], axis=0)
    hi = sdiag.astype(BF).astype(F32)
    sdiag = jnp.where(iota((32, 192), 1) < 96, hi, sdiag - hi).astype(BF)

    def diag_block(a):
        _, _, main, left = GROUPS["own" if a < OWN_BLOCKS else "out"]
        b = a if a < OWN_BLOCKS else a - OWN_BLOCKS
        met = jnp.concatenate([counts[s, 8 * a : 8 * a + 8] for s in range(SIDES)], axis=0)
        hi, lo = split(met)
        d = dot(sdiag, jnp.concatenate([hi, lo, hi, lo], axis=0))
        scale[main + 24 * b : main + 24 * b + 24] = d[0:24]
        scale[left + b : left + b + 1] = d[24:25]

    scale[...] = jnp.zeros_like(scale)
    for a in range(OWN_BLOCKS, BLOCKS):
        diag_block(a)
    post(0, scale)

    mat = material[...]

    def pick(y, width, e):
        m_row = jnp.broadcast_to(mat[:, e], (8, y.shape[1]))[None]
        y = y.reshape(MATS, width // 8, 8, y.shape[1])
        return jnp.where(
            m_row == 0, y[0], jnp.where(m_row == 1, y[1], jnp.where(m_row == 2, y[2], y[3]))
        ).reshape(width, y.shape[3])

    CHUNK = 512
    for c in range(ELEM // CHUNK):
        e = slice(c * CHUNK, (c + 1) * CHUNK)
        y = dot(left3[...], src3[:, e])
        rhs_terms[:, e] = pick(y[0 : MATS * TP], TP, e)
        potential[:, e] = pick(y[MATS * TP :], NP, e)[0:NODES]

    def store_terms(terms, e):
        for s in range(SIDES):
            t = terms[24 * s : 24 * s + 24]
            hi, lo = split(jnp.concatenate([t, t], axis=0))
            t_hi[s, :, e], t_lo[s, :, e] = hi, lo
            t = jnp.broadcast_to(terms[144 + s : 145 + s], (16, terms.shape[1]))
            hi, lo = split(t)
            l_hi[s, :, e], l_lo[s, :, e] = hi, lo

    for c in range(ELEM // CHUNK):
        e = slice(c * CHUNK, (c + 1) * CHUNK)
        store_terms(rhs_terms[:, e], e)

    def row_ids(first, last, dtype):
        r = iota((16, ELEM), 0)
        return jnp.where(r < last - first, r + first, -1).astype(F32).astype(dtype)

    def assemble(name):
        first, last, main, left = GROUPS[name]
        rows = slice(main, left + 16)
        partial[rows] = jnp.zeros((left + 16 - main, 256), F32)

        def add(s, carry):
            hit = row_ids(first, last, BF) == blk_d[s, 0:16]
            hits = [blk_d[s] == BF(a) for a in range(first, last, 2)]
            out = None
            for t, l in ((t_hi, l_hi), (t_lo, l_lo)):
                tv = t[s]
                z = jnp.concatenate(
                    [jnp.where(h, tv, BF(0)) for h in hits] + [jnp.where(hit, l[s], BF(0))], axis=0
                )
                d = dot_nt(z, onehot[s])
                out = d if out is None else out + d
            partial[rows] += out
            return carry

        lax.fori_loop(0, SIDES, add, 0, unroll=True)

    def fetch(name):
        first, last, main, left = GROUPS[name]

        def take(s, carry):
            y = dot(table[main : left + 16], onehot[s]) + dot(table2[main : left + 16], onehot[s])
            blk = blk_f[s]
            if name == "own":
                acc = jnp.zeros((3, 8, ELEM), F32)
                acc_left = jnp.zeros((1, ELEM), F32)
            else:
                acc = x_main[s].reshape(3, 8, ELEM)
                acc_left = x_left[s, 0:1]
            for a in range(first, last):
                ya = y[24 * (a - first) : 24 * (a - first) + 24].reshape(3, 8, ELEM)
                acc = jnp.where((blk == F32(a))[None], ya, acc)
            x_main[s] = acc.reshape(24, ELEM)
            hit = row_ids(first, last, F32).reshape(2, 8, ELEM) == blk[None]
            yl = jnp.where(hit, y[left - main :].reshape(2, 8, ELEM), 0.0)
            x_left[s, 0:1] = acc_left + jnp.sum(yl[0] + yl[1], axis=0, keepdims=True)
            return carry

        lax.fori_loop(0, SIDES, take, 0, unroll=True)

    def gathered():
        rows = [x_main[s] for s in range(SIDES)]
        x = jnp.concatenate([x_left[s, 0:1] for s in range(SIDES)] + [jnp.zeros((10, ELEM), F32)], axis=0)
        x = jnp.concatenate(rows + [x], axis=0)
        hi, lo = split(x)
        x3[0:TP], x3[TP : 2 * TP], x3[2 * TP :] = hi, lo, hi

    def table_rows(name):
        _, _, main, left = GROUPS[name]
        return slice(main, left + 16)

    def update(name, first):
        rows = table_rows(name)
        step = scale[rows] * partial[rows]
        x = step if first else total[rows] + step
        total[rows] = x
        hi, lo = split(x)
        table[rows], table2[rows] = hi, lo

    assemble("out")
    post(1, partial)
    for a in range(OWN_BLOCKS):
        diag_block(a)
    assemble("own")

    def invert(name):
        rows = table_rows(name)
        d = scale[rows]
        scale[rows] = jnp.where(d == 0.0, 0.0, DAMPING / jnp.where(d == 0.0, 1.0, d))

    invert("own")
    update("own", True)
    fetch("own")
    collect(0, scale)
    collect(1, partial)
    invert("out")
    update("out", True)
    fetch("out")

    for sweep in range(SWEEPS - 1):
        gathered()
        for c in range(ELEM // CHUNK):
            e = slice(c * CHUNK, (c + 1) * CHUNK)
            y = pick(dot(a3[...], x3[:, e]), TP, e)
            store_terms(rhs_terms[:, e] - y, e)
        assemble("out")
        post(2 + sweep, partial)
        assemble("own")
        update("own", False)
        fetch("own")
        collect(2 + sweep, partial)
        update("out", False)
        fetch("out")

    rows = slice(OWN_MAIN, OWN_LEFT + 16)
    back = jnp.zeros((304, 256), F32)
    for b in range(3):
        cols = slice(256 * b, 256 * (b + 1))
        r = OUT_MAIN + 24 * (b + 3)
        x = total[r : r + 24]
        xl = jnp.broadcast_to(total[OUT_LEFT + b + 3 : OUT_LEFT + b + 4], (16, 256))
        blk = own_blk[:, cols].astype(F32)
        blk2 = (blk - (iota((48, 256), 0) >= 24).astype(F32)).astype(BF)
        hits = [blk2 == BF(a) for a in range(0, OWN_BLOCKS, 2)]
        r16 = iota((16, 256), 0)
        hit = jnp.where(r16 < OWN_BLOCKS, r16, -1).astype(F32).astype(BF) == blk.astype(BF)
        for xv, lv in zip(split(jnp.concatenate([x, x], axis=0)), split(xl)):
            z = jnp.concatenate(
                [jnp.where(h, xv, BF(0)) for h in hits] + [jnp.where(hit, lv, BF(0))], axis=0
            )
            back = back + dot_nt(z, onehot_out[:, cols])
    full = total[rows] + back
    for a in range(OWN_BLOCKS):
        cols = slice(256 * a, 256 * (a + 1))
        trace_own[0:24, cols] = full[24 * a : 24 * a + 24]
        trace_own[24:25, cols] = full[OWN_LEFT + a : OWN_LEFT + a + 1]

    gathered()
    for c in range(ELEM // CHUNK):
        e = slice(c * CHUNK, (c + 1) * CHUNK)
        y = pick(dot(w3[...], x3[:, e]), NP, e)
        potential[:, e] = potential[:, e] - y[0:NODES]

    for r in range(ROUNDS):
        for k in range(4):
            copy(r, k).wait_send()


def shards(source, inverses, lift, stab, material, face_slot, owner_map):
    vmem = pl.BlockSpec(memory_space=pltpu.VMEM)
    smem = pl.BlockSpec(memory_space=pltpu.SMEM)
    v = pltpu.VMEM
    return pl.pallas_call(
        kernel,
        out_shape=(
            jax.ShapeDtypeStruct((NODES, ELEM), F32),
            jax.ShapeDtypeStruct((FNODES, OWNED), F32),
        ),
        in_specs=[vmem, vmem, vmem, smem, vmem, vmem, vmem],
        out_specs=(vmem, vmem),
        scratch_shapes=[
            v((SIDES, 256, ELEM), BF),
            v((256, GHOSTS), BF),
            v((SIDES, 8, ELEM), F32),
            v((SIDES, 48, ELEM), BF),
            v((SIDES, 16, ELEM), BF),
            v((SIDES, 8 * BLOCKS, 256), F32),
            v((MATS, NP, NP), F32),
            v((256, NP), F32),
            v((NP, ELEM), F32),
            v((3 * NP, ELEM), BF),
            v((MATS * (TP + NP), 3 * NP), BF),
            v((MATS * TP, 3 * TP), BF),
            v((MATS * NP, 3 * TP), BF),
            v((TP, ELEM), F32),
            v((SIDES, 24, ELEM), F32),
            v((SIDES, 8, ELEM), F32),
            v((3 * TP, ELEM), BF),
            v((SIDES, 48, ELEM), BF),
            v((SIDES, 48, ELEM), BF),
            v((SIDES, 16, ELEM), BF),
            v((SIDES, 16, ELEM), BF),
            v((ROWS, 256), F32),
            v((ROWS, 256), F32),
            v((ROWS, 256), BF),
            v((ROWS, 256), BF),
            v((ROWS, 256), F32),
            v((ROUNDS, 2, SENT, CAP_W), F32),
            v((ROUNDS, 2, SENT, CAP_W), F32),
            v((ROUNDS, 2, SENT, CAP_N), F32),
            v((ROUNDS, 2, SENT, CAP_N), F32),
            pltpu.SemaphoreType.DMA((ROUNDS, 4)),
            pltpu.SemaphoreType.DMA((ROUNDS, 4)),
        ],
        compiler_params=pltpu.CompilerParams(
            collective_id=0, has_side_effects=True, vmem_limit_bytes=48 * 2**20
        ),
    )(
        source,
        inverses.transpose(1, 0, 2),
        lift.T,
        stab,
        material.reshape(1, ELEM),
        face_slot,
        owner_map,
    )


def solution(mesh):
    both = ("wide", "narrow")
    return jax.shard_map(
        shards,
        mesh=mesh,
        in_specs=(
            P(None, both), P(), P(), P(), P(both), P(None, both), P(both, None),
        ),
        out_specs=(P(None, both), P(None, both)),
        check_vma=False,
    )
```

```python
import functools

import jax
import jax.numpy as jnp
from jax import lax
from jax.experimental import pallas as pl
from jax.experimental.pallas import tpu as pltpu
from jax.sharding import PartitionSpec as P

MESH = pl.DeviceIdType.MESH
F32, BF, F8 = jnp.float32, jnp.bfloat16, jnp.float8_e4m3fn
FULL = 3500.0
HIGH = lax.Precision.HIGHEST
DAMPING = 0.6
SWEEPS = 3

NODES, FNODES, SIDES, MATS = 125, 25, 6, 4
ELEM = 1024
OWNED = 3 * ELEM
CAP_W, CAP_N = 256, 128
GHOSTS = 2 * CAP_W + 2 * CAP_N
TP = 160
NP = 128

OWN_BLOCKS, BLOCKS = 12, 18
OWN_MAIN, OWN_LEFT, OUT_MAIN, OUT_LEFT, ROWS = 0, 288, 320, 464, 480
GROUPS = {
    "own": (0, 12, OWN_MAIN, OWN_LEFT, slice(0, 320)),
    "out": (12, 18, OUT_MAIN, OUT_LEFT, slice(320, 480)),
}
WEIGHTS = (16.0, 1.0, 0.0625)
SENT = 56
ROUNDS = 2 + SWEEPS - 1


def dot(a, b, precision=None):
    return jnp.dot(a, b, precision=precision, preferred_element_type=F32)


def dot_nt(a, b, precision=None):
    return lax.dot_general(
        a, b, (((1,), (1,)), ((), ())), precision=precision, preferred_element_type=F32
    )


def split(x):
    hi = x.astype(BF)
    return hi, (x - hi.astype(F32)).astype(BF)


def split8(v):
    a = (v * 0.0625).astype(F8)
    r = v - 16.0 * a.astype(F32)
    b = r.astype(F8)
    c = ((r - b.astype(F32)) * 16.0).astype(F8)
    return a, b, c


def scaling(x):
    m = jnp.max(jnp.max(jnp.abs(x), axis=0, keepdims=True), axis=1, keepdims=True)
    m = jnp.maximum(m, 1e-30)
    return FULL / m, m * (1.0 / FULL)


def iota(shape, dim):
    return lax.broadcasted_iota(jnp.int32, shape, dim)


def trace_position(p):
    side = jnp.zeros_like(p)
    for i in range(1, SIDES):
        side = side + (p >= 24 * i).astype(jnp.int32)
    node = jnp.where(p < 144, p - 24 * side, 24)
    side = jnp.where(p < 144, side, p - 144)
    return side, node


def kernel(
    source_hbm, inverses_hbm, lift_hbm, stab_hbm, material_hbm, face_slot_hbm, owner_map_hbm,
    potential, trace_own,
    source, inverses, lift, stab, material, face_slot, owner_map,
    onehot, onehot_out, blk_f, blk_d, idx_f, counts,
    inv_pad, lift_pad, src_pad, src3, left3, a3, w3,
    rhs_terms, terms, x_main, x_left, x3, t_parts, l_parts,
    partial, total, table, scale,
    send_w, recv_w, send_n, recv_n, send_sems, recv_sems, in_sems,
):
    loads = [
        pltpu.make_async_copy(src, dst, in_sems.at[i])
        for i, (src, dst) in enumerate(
            (
                (face_slot_hbm, face_slot),
                (owner_map_hbm, owner_map),
                (material_hbm, material),
                (inverses_hbm, inverses),
                (lift_hbm, lift),
                (stab_hbm, stab),
                (source_hbm, source),
            )
        )
    ]
    for load in loads:
        load.start()
    w, n = lax.axis_index("wide"), lax.axis_index("narrow")
    wide, narrow = lax.axis_size("wide"), lax.axis_size("narrow")
    ends = (w == 0, w == wide - 1, n == 0, n == narrow - 1)
    one = (w ^ 1, n ^ 1)
    neighbour = (
        (jnp.where(ends[0], w, w - 1), jnp.where(ends[0], one[1], n)),
        (jnp.where(ends[1], w, w + 1), jnp.where(ends[1], one[1], n)),
        (jnp.where(ends[2], one[0], w), jnp.where(ends[2], n, n - 1)),
        (jnp.where(ends[3], one[0], w), jnp.where(ends[3], n, n + 1)),
    )
    barrier = pltpu.get_barrier_semaphore()
    for k in range(4):
        pl.semaphore_signal(barrier, inc=1, device_id=neighbour[k], device_id_type=MESH)
    pl.semaphore_wait(barrier, 4)

    def buffers(k):
        return (send_w, recv_w, k) if k < 2 else (send_n, recv_n, k - 2)

    def copy(r, k):
        send, recv, side = buffers(k)
        return pltpu.make_async_remote_copy(
            src_ref=send.at[r, side],
            dst_ref=recv.at[r, jnp.where(ends[k], side, 1 - side)],
            send_sem=send_sems.at[r, k],
            recv_sem=recv_sems.at[r, jnp.where(ends[k], k, k ^ 1)],
            device_id=neighbour[k],
            device_id_type=MESH,
        )

    def arrival(r, k):
        send, recv, side = buffers(k)
        return pltpu.make_async_remote_copy(
            src_ref=send.at[r, side],
            dst_ref=recv.at[r, side],
            send_sem=send_sems.at[r, k],
            recv_sem=recv_sems.at[r, k],
            device_id=neighbour[k],
            device_id_type=MESH,
        )

    def places(k):
        block = min(k, 2)
        lo, width = (0, CAP_W) if k < 2 else ((k - 2) * CAP_N, CAP_N)
        return block, slice(lo, lo + width)

    def post(r, values):
        for k in range(4):
            send, recv, side = buffers(k)
            block, cols = places(k)
            ghost, shared = OUT_MAIN + 24 * block, OUT_MAIN + 24 * (block + 3)
            send[r, side, 0:24] = values[ghost : ghost + 24, cols]
            send[r, side, 24:48] = values[shared : shared + 24, cols]
            ghost, shared = OUT_LEFT + block, OUT_LEFT + block + 3
            send[r, side, 48:49] = values[ghost : ghost + 1, cols]
            send[r, side, 49:50] = values[shared : shared + 1, cols]

            copy(r, k).start()

    def collect(r, values):
        for k in range(4):
            arrival(r, k).wait_recv()

        for k in range(4):
            send, recv, side = buffers(k)
            block, cols = places(k)
            ghost, shared = OUT_MAIN + 24 * block, OUT_MAIN + 24 * (block + 3)
            values[shared : shared + 24, cols] += recv[r, side, 0:24]
            values[ghost : ghost + 24, cols] += recv[r, side, 24:48]
            ghost, shared = OUT_LEFT + block, OUT_LEFT + block + 3
            values[shared : shared + 1, cols] += recv[r, side, 48:49]
            values[ghost : ghost + 1, cols] += recv[r, side, 49:50]

    for load in loads[:3]:
        load.wait()
    owners = owner_map[...]
    own_blk, own_col = owners >> 8, owners & 255
    place = iota((1, GHOSTS), 1) + 1
    onehot_out[...] = (iota((256, GHOSTS), 0) == own_col).astype(F32).astype(BF)
    row16 = iota((16, GHOSTS), 0)
    named = jnp.where(row16 < OWN_BLOCKS, row16, -1) == own_blk
    digits = jnp.concatenate(
        [
            jnp.where(named, (place >> 8).astype(F32), 0.0),
            jnp.where(named, (place & 255).astype(F32), 0.0),
        ],
        axis=0,
    ).astype(BF)
    place_table = dot_nt(digits, onehot_out[...]).astype(BF)

    def renumber(s, carry):
        v = face_slot[pl.ds(s, 1), :]
        col = jnp.broadcast_to(v & 255, (256, ELEM))
        first = (iota((256, ELEM), 0) == col).astype(F32).astype(BF)
        found = dot(place_table, first)
        hit = iota((16, ELEM), 0) == (v >> 8)
        spot = jnp.sum(
            jnp.where(hit, 256.0 * found[0:16] + found[16:32], 0.0), axis=0, keepdims=True
        ).astype(jnp.int32)
        v = jnp.where(spot > 0, OWNED + GHOSTS - 1 + spot, v)
        met = iota((256, ELEM), 0) == (v & 255)
        for p, weight in enumerate(WEIGHTS):
            onehot[p, s] = jnp.where(met, weight, 0.0).astype(F8)
        blk = (v >> 8).astype(F32)
        blk_f[s] = jnp.broadcast_to(blk, (8, ELEM))
        blk_d[s] = (blk - (iota((48, ELEM), 0) >= 24).astype(F32)).astype(BF)
        idx = 8.0 * blk + material[...].astype(F32)
        idx_f[s] = (idx - iota((16, ELEM), 0).astype(F32)).astype(BF)
        return carry

    lax.fori_loop(0, SIDES, renumber, 0, unroll=True)

    def count(s, carry):
        idx = idx_f[s]
        ones = jnp.concatenate(
            [
                jnp.where(idx == BF(16 * t), BF(1), BF(0))
                for t in range(10)
            ],
            axis=0,
        )
        counts[s] = dot_nt(ones.astype(F8), onehot[1, s])
        return carry

    lax.fori_loop(0, SIDES, count, 0, unroll=True)

    for load in loads[3:]:
        load.wait()
    inv_pad[...] = jnp.zeros_like(inv_pad)
    for m in range(MATS):
        inv_pad[m, 0:NODES, 0:NODES] = inverses[:, m, :]
    lift_pad[...] = jnp.zeros_like(lift_pad)
    lift_pad[0 : SIDES * FNODES, 0:NODES] = lift[...]
    src_pad[...] = jnp.zeros_like(src_pad)
    src_pad[0:NODES] = source[...]
    hi, lo = split(src_pad[...])
    src3[0:NP], src3[NP : 2 * NP], src3[2 * NP :] = hi, lo, hi

    side_p, node_p = trace_position(iota((TP, 256), 0))
    order = jnp.where(side_p < SIDES, 6 * node_p + side_p, -1)
    perm = (iota((TP, 256), 1) == order).astype(F32)
    lift_t = dot(perm, lift_pad[...], HIGH)
    eye = iota((TP, TP), 0) == iota((TP, TP), 1)
    col = iota((TP, 192), 1)
    for i in range(1, 4):
        col = col - 48 * (iota((TP, 192), 1) >= 48 * i).astype(jnp.int32)
    side_c, _ = trace_position(iota((TP, 192), 0))
    spread = jnp.zeros((TP, 192), F32)
    for m in range(MATS):
        inv = inv_pad[m]
        wm = dot_nt(inv, lift_t, HIGH)
        wt = dot(lift_t, inv, HIGH)
        am = dot_nt(wt, lift_t, HIGH)
        diagonal = jnp.abs(jnp.sum(jnp.where(eye, am, 0.0), axis=1, keepdims=True)) + stab[0:1, m : m + 1]
        spread = spread + jnp.where(col == 8 * side_c + m, diagonal, 0.0)
        am = am + jnp.where(eye, stab[0:1, m : m + 1], 0.0)
        hi, lo = split(am)
        a3[TP * m : TP * (m + 1)] = jnp.concatenate([hi, hi, lo], axis=1)
        hi, lo = split(wm)
        w3[NP * m : NP * (m + 1)] = jnp.concatenate([hi, hi, lo], axis=1)
        hi, lo = split(wt)
        r = slice(TP * m, TP * (m + 1))
        left3[r, 0:NP], left3[r, NP : 2 * NP], left3[r, 2 * NP :] = hi, hi, lo
        hi, lo = split(inv)
        r = slice(MATS * TP + NP * m, MATS * TP + NP * (m + 1))
        left3[r, 0:NP], left3[r, NP : 2 * NP], left3[r, 2 * NP :] = hi, hi, lo
    sdiag = jnp.zeros((24, 192), F32)
    for s in range(SIDES):
        sdiag = sdiag + spread[24 * s : 24 * s + 24]
    last = jnp.sum(spread[144:152], axis=0, keepdims=True)
    sdiag = jnp.concatenate([sdiag, jnp.broadcast_to(last, (8, 192))], axis=0)
    hi = sdiag.astype(BF).astype(F32)
    sdiag = jnp.where(iota((32, 192), 1) < 96, hi, sdiag - hi).astype(BF)

    def diag_block(a):
        _, _, main, left, _ = GROUPS["own" if a < OWN_BLOCKS else "out"]
        b = a if a < OWN_BLOCKS else a - OWN_BLOCKS
        met = jnp.concatenate([counts[s, 8 * a : 8 * a + 8] for s in range(SIDES)], axis=0)
        hi, lo = split(met)
        d = dot(sdiag, jnp.concatenate([hi, lo, hi, lo], axis=0))
        scale[main + 24 * b : main + 24 * b + 24] = d[0:24]
        scale[left + b : left + b + 1] = d[24:25]

    scale[...] = jnp.zeros_like(scale)
    for a in range(OWN_BLOCKS, BLOCKS):
        diag_block(a)
    post(0, scale)

    mat = material[...]

    def pick(y, width, e):
        m_row = jnp.broadcast_to(mat[:, e], (8, y.shape[1]))[None]
        y = y.reshape(MATS, width // 8, 8, y.shape[1])
        return jnp.where(
            m_row == 0, y[0], jnp.where(m_row == 1, y[1], jnp.where(m_row == 2, y[2], y[3]))
        ).reshape(width, y.shape[3])

    CHUNK = 512
    for c in range(ELEM // CHUNK):
        e = slice(c * CHUNK, (c + 1) * CHUNK)
        y = dot(left3[...], src3[:, e])
        rhs_terms[:, e] = pick(y[0 : MATS * TP], TP, e)
        potential[:, e] = pick(y[MATS * TP :], NP, e)[0:NODES]

    def store_terms(source_terms):
        up, down = scaling(source_terms[...])
        for s in range(SIDES):
            t = source_terms[24 * s : 24 * s + 24] * up
            l = jnp.broadcast_to(source_terms[144 + s : 145 + s] * up, (16, ELEM))
            for p, part in enumerate(split8(jnp.concatenate([t, t], axis=0))):
                t_parts[p, s] = part.astype(BF)
            for p, part in enumerate(split8(l)):
                l_parts[p, s] = part.astype(BF)
        return down

    terms_down = store_terms(rhs_terms)

    def row_ids(first, last, dtype):
        r = iota((16, ELEM), 0)
        return jnp.where(r < last - first, r + first, -1).astype(F32).astype(dtype)

    def assemble(name, down):
        first, last, _, _, rows = GROUPS[name]
        out = None
        for s in range(SIDES):
            hit = row_ids(first, last, BF) == blk_d[s, 0:16]
            hits = [blk_d[s] == BF(a) for a in range(first, last, 2)]
            for p in range(3):
                t = t_parts[p, s]
                z = [jnp.where(h, t, BF(0)) for h in hits]
                z.append(jnp.where(hit, l_parts[p, s], BF(0)))
                if name == "own":
                    z.append(jnp.zeros((16, ELEM), BF))
                d = dot_nt(jnp.concatenate(z, axis=0).astype(F8), onehot[p, s])
                out = d if out is None else out + d
        partial[rows] = out * down

    def fetch(name, down):
        first, last, main, left, rows = GROUPS[name]
        for s in range(SIDES):
            y = dot(table[0, rows], onehot[0, s])
            for p in (1, 2):
                y = y + dot(table[p, rows], onehot[p, s])
            blk = blk_f[s]
            acc = jnp.zeros((3, 8, ELEM), F32)
            for a in range(first, last):
                ya = y[24 * (a - first) : 24 * (a - first) + 24].reshape(3, 8, ELEM)
                acc = jnp.where((blk == F32(a))[None], ya, acc)
            acc = acc.reshape(24, ELEM) * down
            hit = row_ids(first, last, F32).reshape(2, 8, ELEM) == blk[None]
            yl = jnp.where(hit, y[left - main : left - main + 16].reshape(2, 8, ELEM), 0.0)
            acc_left = jnp.sum(yl[0] + yl[1], axis=0, keepdims=True) * down
            if name == "out":
                acc = acc + x_main[s]
                acc_left = acc_left + x_left[s, 0:1]
            x_main[s] = acc
            x_left[s, 0:1] = acc_left

    def gathered():
        rows = [x_main[s] for s in range(SIDES)]
        x = jnp.concatenate([x_left[s, 0:1] for s in range(SIDES)] + [jnp.zeros((10, ELEM), F32)], axis=0)
        x = jnp.concatenate(rows + [x], axis=0)
        hi, lo = split(x)
        x3[0:TP], x3[TP : 2 * TP], x3[2 * TP :] = hi, lo, hi

    def update(name, first):
        rows = GROUPS[name][4]
        step = scale[rows] * partial[rows]
        x = step if first else total[rows] + step
        total[rows] = x
        up, down = scaling(x)
        for p, part in enumerate(split8(x * up)):
            table[p, rows] = part
        return down

    assemble("out", terms_down)
    post(1, partial)
    for a in range(OWN_BLOCKS):
        diag_block(a)
    assemble("own", terms_down)

    def invert(name):
        rows = GROUPS[name][4]
        d = scale[rows]
        scale[rows] = jnp.where(d == 0.0, 0.0, DAMPING / jnp.where(d == 0.0, 1.0, d))

    invert("own")
    fetch("own", update("own", True))
    collect(0, scale)
    collect(1, partial)
    invert("out")
    fetch("out", update("out", True))

    for sweep in range(SWEEPS - 1):
        gathered()
        for c in range(ELEM // CHUNK):
            e = slice(c * CHUNK, (c + 1) * CHUNK)
            y = pick(dot(a3[...], x3[:, e]), TP, e)
            terms[:, e] = rhs_terms[:, e] - y
        terms_down = store_terms(terms)
        assemble("out", terms_down)
        post(2 + sweep, partial)
        assemble("own", terms_down)
        fetch("own", update("own", False))
        collect(2 + sweep, partial)
        fetch("out", update("out", False))

    rows = slice(OWN_MAIN, OWN_LEFT + 16)
    back = jnp.zeros((304, 256), F32)
    for b in range(3):
        cols = slice(256 * b, 256 * (b + 1))
        r = OUT_MAIN + 24 * (b + 3)
        x = total[r : r + 24]
        xl = jnp.broadcast_to(total[OUT_LEFT + b + 3 : OUT_LEFT + b + 4], (16, 256))
        blk = own_blk[:, cols].astype(F32)
        blk2 = (blk - (iota((48, 256), 0) >= 24).astype(F32)).astype(BF)
        hits = [blk2 == BF(a) for a in range(0, OWN_BLOCKS, 2)]
        r16 = iota((16, 256), 0)
        hit = jnp.where(r16 < OWN_BLOCKS, r16, -1).astype(F32).astype(BF) == blk.astype(BF)
        for xv, lv in zip(split(jnp.concatenate([x, x], axis=0)), split(xl)):
            z = jnp.concatenate(
                [jnp.where(h, xv, BF(0)) for h in hits] + [jnp.where(hit, lv, BF(0))], axis=0
            )
            back = back + dot_nt(z, onehot_out[:, cols])
    full = total[rows] + back
    for a in range(OWN_BLOCKS):
        cols = slice(256 * a, 256 * (a + 1))
        trace_own[0:24, cols] = full[24 * a : 24 * a + 24]
        trace_own[24:25, cols] = full[OWN_LEFT + a : OWN_LEFT + a + 1]

    gathered()
    for c in range(ELEM // CHUNK):
        e = slice(c * CHUNK, (c + 1) * CHUNK)
        y = pick(dot(w3[...], x3[:, e]), NP, e)
        potential[:, e] = potential[:, e] - y[0:NODES]

    for r in range(ROUNDS):
        for k in range(4):
            copy(r, k).wait_send()


def shards(source, inverses, lift, stab, material, face_slot, owner_map):
    vmem = pl.BlockSpec(memory_space=pltpu.VMEM)
    hbm = pl.BlockSpec(memory_space=pltpu.HBM)
    v = pltpu.VMEM
    return pl.pallas_call(
        kernel,
        out_shape=(
            jax.ShapeDtypeStruct((NODES, ELEM), F32),
            jax.ShapeDtypeStruct((FNODES, OWNED), F32),
        ),
        in_specs=[hbm] * 7,
        out_specs=(vmem, vmem),
        scratch_shapes=[
            v((NODES, ELEM), F32),
            v((NODES, MATS, NODES), F32),
            v((SIDES * FNODES, NODES), F32),
            v((1, MATS), F32),
            v((1, ELEM), jnp.int32),
            v((SIDES, ELEM), jnp.int32),
            v((1, GHOSTS), jnp.int32),
            v((3, SIDES, 256, ELEM), F8),
            v((256, GHOSTS), BF),
            v((SIDES, 8, ELEM), F32),
            v((SIDES, 48, ELEM), BF),
            v((SIDES, 16, ELEM), BF),
            v((SIDES, 160, 256), F32),
            v((MATS, NP, NP), F32),
            v((256, NP), F32),
            v((NP, ELEM), F32),
            v((3 * NP, ELEM), BF),
            v((MATS * (TP + NP), 3 * NP), BF),
            v((MATS * TP, 3 * TP), BF),
            v((MATS * NP, 3 * TP), BF),
            v((TP, ELEM), F32),
            v((TP, ELEM), F32),
            v((SIDES, 24, ELEM), F32),
            v((SIDES, 8, ELEM), F32),
            v((3 * TP, ELEM), BF),
            v((3, SIDES, 48, ELEM), BF),
            v((3, SIDES, 16, ELEM), BF),
            v((ROWS, 256), F32),
            v((ROWS, 256), F32),
            v((3, ROWS, 256), F8),
            v((ROWS, 256), F32),
            v((ROUNDS, 2, SENT, CAP_W), F32),
            v((ROUNDS, 2, SENT, CAP_W), F32),
            v((ROUNDS, 2, SENT, CAP_N), F32),
            v((ROUNDS, 2, SENT, CAP_N), F32),
            pltpu.SemaphoreType.DMA((ROUNDS, 4)),
            pltpu.SemaphoreType.DMA((ROUNDS, 4)),
            pltpu.SemaphoreType.DMA((7,)),
        ],
        compiler_params=pltpu.CompilerParams(
            collective_id=0, has_side_effects=True, vmem_limit_bytes=63 * 2**20
        ),
    )(
        source,
        inverses.transpose(1, 0, 2),
        lift.T,
        stab.reshape(1, MATS),
        material.reshape(1, ELEM),
        face_slot,
        owner_map,
    )


def solution(mesh):
    both = ("wide", "narrow")
    return jax.shard_map(
        shards,
        mesh=mesh,
        in_specs=(
            P(None, both), P(), P(), P(), P(both), P(None, both), P(both, None),
        ),
        out_specs=(P(None, both), P(None, both)),
        check_vma=False,
    )
```

```python
import functools

import jax
import jax.numpy as jnp
from jax import lax
from jax.experimental import pallas as pl
from jax.experimental.pallas import tpu as pltpu
from jax.sharding import PartitionSpec as P

MESH = pl.DeviceIdType.MESH
F32, BF, F8 = jnp.float32, jnp.bfloat16, jnp.float8_e4m3fn
FULL = 3500.0
DAMPING = 0.6
SWEEPS = 3

NODES, FNODES, SIDES, MATS = 125, 25, 6, 4
ELEM = 1024
OWNED = 3 * ELEM
CAP_W, CAP_N = 256, 128
GHOSTS = 2 * CAP_W + 2 * CAP_N
TP = 160
NP = 128

OWN_BLOCKS, BLOCKS = 12, 18
OWN_MAIN, OWN_LEFT, OUT_MAIN, OUT_LEFT, ROWS = 0, 288, 320, 464, 480
GROUPS = {
    "own": (0, 12, OWN_MAIN, OWN_LEFT, slice(0, 320)),
    "out": (12, 18, OUT_MAIN, OUT_LEFT, slice(320, 480)),
}
WEIGHTS = (16.0, 1.0, 0.0625)
SENT = 56
ROUNDS = 2 + SWEEPS - 1


def dot(a, b, precision=None):
    return jnp.dot(a, b, precision=precision, preferred_element_type=F32)


def dot_nt(a, b, precision=None):
    return lax.dot_general(
        a, b, (((1,), (1,)), ((), ())), precision=precision, preferred_element_type=F32
    )


def split(x):
    hi = x.astype(BF)
    return hi, (x - hi.astype(F32)).astype(BF)


def split8(v):
    a = (v * 0.0625).astype(F8)
    r = v - 16.0 * a.astype(F32)
    b = r.astype(F8)
    c = ((r - b.astype(F32)) * 16.0).astype(F8)
    return a, b, c


def dot3(a, b, product):
    return product(a[0], b[0]) + (product(a[0], b[1]) + product(a[1], b[0]))


def largest(x):
    return jnp.max(jnp.max(jnp.abs(x), axis=0, keepdims=True), axis=1, keepdims=True)


def factors(m):
    m = jnp.maximum(m, 1e-30)
    return FULL / m, m * (1.0 / FULL)


def iota(shape, dim):
    return lax.broadcasted_iota(jnp.int32, shape, dim)


def trace_position(p):
    side = jnp.zeros_like(p)
    for i in range(1, SIDES):
        side = side + (p >= 24 * i).astype(jnp.int32)
    node = jnp.where(p < 144, p - 24 * side, 24)
    side = jnp.where(p < 144, side, p - 144)
    return side, node


def kernel(
    source_hbm, inverses_hbm, lift_hbm, stab_hbm, material_hbm, face_slot_hbm, owner_map_hbm,
    potential, trace_own,
    source, inverses, lift, stab, material, face_slot, owner_map,
    onehot, onehot_out, blk_f, blk_d, idx_f, counts,
    inv_pad, lift_pad, src_pad, src3, left3, a3, w3,
    rhs_terms, x_main, x_left, x3, t_parts, l_parts,
    partial, total, table, scale,
    send_w, recv_w, send_n, recv_n, send_sems, recv_sems, in_sems,
):
    loads = [
        pltpu.make_async_copy(src, dst, in_sems.at[i])
        for i, (src, dst) in enumerate(
            (
                (face_slot_hbm, face_slot),
                (owner_map_hbm, owner_map),
                (material_hbm, material),
                (inverses_hbm, inverses),
                (lift_hbm, lift),
                (stab_hbm, stab),
                (source_hbm, source),
            )
        )
    ]
    for load in loads:
        load.start()
    w, n = lax.axis_index("wide"), lax.axis_index("narrow")
    wide, narrow = lax.axis_size("wide"), lax.axis_size("narrow")
    ends = (w == 0, w == wide - 1, n == 0, n == narrow - 1)
    one = (w ^ 1, n ^ 1)
    neighbour = (
        (jnp.where(ends[0], w, w - 1), jnp.where(ends[0], one[1], n)),
        (jnp.where(ends[1], w, w + 1), jnp.where(ends[1], one[1], n)),
        (jnp.where(ends[2], one[0], w), jnp.where(ends[2], n, n - 1)),
        (jnp.where(ends[3], one[0], w), jnp.where(ends[3], n, n + 1)),
    )
    barrier = pltpu.get_barrier_semaphore()
    for k in range(4):
        pl.semaphore_signal(barrier, inc=1, device_id=neighbour[k], device_id_type=MESH)

    def buffers(k):
        return (send_w, recv_w, k) if k < 2 else (send_n, recv_n, k - 2)

    def copy(r, k):
        send, recv, side = buffers(k)
        return pltpu.make_async_remote_copy(
            src_ref=send.at[r, side],
            dst_ref=recv.at[r, jnp.where(ends[k], side, 1 - side)],
            send_sem=send_sems.at[r, k],
            recv_sem=recv_sems.at[r, jnp.where(ends[k], k, k ^ 1)],
            device_id=neighbour[k],
            device_id_type=MESH,
        )

    def arrival(r, k):
        send, recv, side = buffers(k)
        return pltpu.make_async_remote_copy(
            src_ref=send.at[r, side],
            dst_ref=recv.at[r, side],
            send_sem=send_sems.at[r, k],
            recv_sem=recv_sems.at[r, k],
            device_id=neighbour[k],
            device_id_type=MESH,
        )

    def places(k):
        block = min(k, 2)
        lo, width = (0, CAP_W) if k < 2 else ((k - 2) * CAP_N, CAP_N)
        return block, slice(lo, lo + width)

    def post(r, values):
        for k in range(4):
            send, recv, side = buffers(k)
            block, cols = places(k)
            ghost, shared = OUT_MAIN + 24 * block, OUT_MAIN + 24 * (block + 3)
            send[r, side, 0:24] = values[ghost : ghost + 24, cols]
            send[r, side, 24:48] = values[shared : shared + 24, cols]
            ghost, shared = OUT_LEFT + block, OUT_LEFT + block + 3
            send[r, side, 48:49] = values[ghost : ghost + 1, cols]
            send[r, side, 49:50] = values[shared : shared + 1, cols]

            copy(r, k).start()

    def collect(r, values):
        for k in range(4):
            arrival(r, k).wait_recv()

        for k in range(4):
            send, recv, side = buffers(k)
            block, cols = places(k)
            ghost, shared = OUT_MAIN + 24 * block, OUT_MAIN + 24 * (block + 3)
            values[shared : shared + 24, cols] += recv[r, side, 0:24]
            values[ghost : ghost + 24, cols] += recv[r, side, 24:48]
            ghost, shared = OUT_LEFT + block, OUT_LEFT + block + 3
            values[shared : shared + 1, cols] += recv[r, side, 48:49]
            values[ghost : ghost + 1, cols] += recv[r, side, 49:50]

    for load in loads[:3]:
        load.wait()
    owners = owner_map[...]
    own_blk, own_col = owners >> 8, owners & 255
    place = iota((1, GHOSTS), 1) + 1
    onehot_out[...] = (iota((256, GHOSTS), 0) == own_col).astype(F32).astype(BF)
    row16 = iota((16, GHOSTS), 0)
    named = jnp.where(row16 < OWN_BLOCKS, row16, -1) == own_blk
    digits = jnp.concatenate(
        [
            jnp.where(named, (place >> 8).astype(F32), 0.0),
            jnp.where(named, (place & 255).astype(F32), 0.0),
        ],
        axis=0,
    ).astype(BF)
    place_table = dot_nt(digits, onehot_out[...]).astype(BF)

    def renumber(s, carry):
        v = face_slot[pl.ds(s, 1), :]
        row = iota((256, ELEM), 0).astype(F32).astype(BF)
        first = jnp.where(row == (v & 255).astype(F32).astype(BF), BF(1), BF(0))
        found = dot(place_table, first)
        hit = iota((16, ELEM), 0) == (v >> 8)
        spot = jnp.sum(
            jnp.where(hit, 256.0 * found[0:16] + found[16:32], 0.0), axis=0, keepdims=True
        ).astype(jnp.int32)
        v = jnp.where(spot > 0, OWNED + GHOSTS - 1 + spot, v)
        met = row == (v & 255).astype(F32).astype(BF)
        for p, weight in enumerate(WEIGHTS):
            onehot[p, s] = jnp.where(met, BF(weight), BF(0)).astype(F8)
        blk = (v >> 8).astype(F32)
        blk_f[s] = jnp.broadcast_to(blk, (8, ELEM))
        blk_d[s] = (blk - (iota((48, ELEM), 0) >= 24).astype(F32)).astype(BF)
        idx = 8.0 * blk + material[...].astype(F32)
        idx_f[s] = (idx - iota((16, ELEM), 0).astype(F32)).astype(BF)
        return carry

    lax.fori_loop(0, SIDES, renumber, 0, unroll=True)

    def count(s, carry):
        idx = idx_f[s]
        ones = jnp.concatenate(
            [
                jnp.where(idx == BF(16 * t), BF(1), BF(0))
                for t in range(10)
            ],
            axis=0,
        )
        counts[s] = dot_nt(ones.astype(F8), onehot[1, s])
        return carry

    lax.fori_loop(0, SIDES, count, 0, unroll=True)

    for load in loads[3:]:
        load.wait()
    inv_pad[...] = jnp.zeros_like(inv_pad)
    for m in range(MATS):
        inv_pad[m, 0:NODES, 0:NODES] = inverses[:, m, :]
    lift_pad[...] = jnp.zeros_like(lift_pad)
    lift_pad[0 : SIDES * FNODES, 0:NODES] = lift[...]
    src_pad[...] = jnp.zeros_like(src_pad)
    src_pad[0:NODES] = source[...]
    hi, lo = split(src_pad[...])
    src3[0:NP], src3[NP : 2 * NP], src3[2 * NP :] = hi, lo, hi

    side_p, node_p = trace_position(iota((TP, 256), 0))
    order = jnp.where(side_p < SIDES, 6 * node_p + side_p, -1)
    perm = (iota((TP, 256), 1) == order).astype(F32).astype(BF)
    hi, lo = split(lift_pad[...])
    last = (lift_pad[...] - hi.astype(F32) - lo.astype(F32)).astype(BF)
    lift_t = split(dot(perm, hi) + dot(perm, lo) + dot(perm, last))
    row_sum = jnp.zeros((TP, 1), F32)
    eye = iota((TP, TP), 0) == iota((TP, TP), 1)
    col = iota((TP, 192), 1)
    for i in range(1, 4):
        col = col - 48 * (iota((TP, 192), 1) >= 48 * i).astype(jnp.int32)
    side_c, _ = trace_position(iota((TP, 192), 0))
    spread = jnp.zeros((TP, 192), F32)
    for m in range(MATS):
        inv = split(inv_pad[m])
        wt = dot3(lift_t, inv, dot)
        am = dot3(split(wt), lift_t, dot_nt)
        diagonal = jnp.abs(jnp.sum(jnp.where(eye, am, 0.0), axis=1, keepdims=True)) + stab[0:1, m : m + 1]
        spread = spread + jnp.where(col == 8 * side_c + m, diagonal, 0.0)
        am = am + jnp.where(eye, stab[0:1, m : m + 1], 0.0)
        hi, lo = split(am)
        a3[TP * m : TP * (m + 1)] = jnp.concatenate([hi, hi, lo], axis=1)
        row_sum = jnp.maximum(row_sum, jnp.sum(jnp.abs(am), axis=1, keepdims=True))
        hi, lo = split(wt)
        r = slice(TP * m, TP * (m + 1))
        left3[r, 0:NP], left3[r, NP : 2 * NP], left3[r, 2 * NP :] = hi, hi, lo
        hi, lo = inv
        r = slice(MATS * TP + NP * m, MATS * TP + NP * (m + 1))
        left3[r, 0:NP], left3[r, NP : 2 * NP], left3[r, 2 * NP :] = hi, hi, lo
    sdiag = jnp.zeros((24, 192), F32)
    for s in range(SIDES):
        sdiag = sdiag + spread[24 * s : 24 * s + 24]
    last = jnp.sum(spread[144:152], axis=0, keepdims=True)
    sdiag = jnp.concatenate([sdiag, jnp.broadcast_to(last, (8, 192))], axis=0)
    hi = sdiag.astype(BF).astype(F32)
    sdiag = jnp.where(iota((32, 192), 1) < 96, hi, sdiag - hi).astype(BF)

    def diag_block(a):
        _, _, main, left, _ = GROUPS["own" if a < OWN_BLOCKS else "out"]
        b = a if a < OWN_BLOCKS else a - OWN_BLOCKS
        met = jnp.concatenate([counts[s, 8 * a : 8 * a + 8] for s in range(SIDES)], axis=0)
        hi, lo = split(met)
        d = dot(sdiag, jnp.concatenate([hi, lo, hi, lo], axis=0))
        scale[main + 24 * b : main + 24 * b + 24] = d[0:24]
        scale[left + b : left + b + 1] = d[24:25]

    mat = material[...]

    def pick(y, width, e):
        m_row = jnp.broadcast_to(mat[:, e], (8, y.shape[1]))[None]
        y = y.reshape(MATS, width // 8, 8, y.shape[1])
        return jnp.where(
            m_row == 0, y[0], jnp.where(m_row == 1, y[1], jnp.where(m_row == 2, y[2], y[3]))
        ).reshape(width, y.shape[3])

    CHUNK = 512
    for c in range(ELEM // CHUNK):
        e = slice(c * CHUNK, (c + 1) * CHUNK)
        rhs_terms[:, e] = pick(dot(left3[0 : MATS * TP], src3[:, e]), TP, e)

    def store_terms(values, e, up):
        width = values.shape[1]
        for s in range(SIDES):
            t = values[24 * s : 24 * s + 24] * up
            l = jnp.broadcast_to(values[144 + s : 145 + s] * up, (16, width))
            for p, part in enumerate(split8(jnp.concatenate([t, t], axis=0))):
                t_parts[p, s, :, e] = part.astype(BF)
            for p, part in enumerate(split8(l)):
                l_parts[p, s, :, e] = part.astype(BF)

    rhs_max = largest(rhs_terms[...])
    gain = largest(row_sum)
    terms_up, terms_down = factors(rhs_max)
    for c in range(ELEM // CHUNK):
        e = slice(c * CHUNK, (c + 1) * CHUNK)
        store_terms(rhs_terms[:, e], e, terms_up)

    def row_ids(first, last, dtype):
        r = iota((16, ELEM), 0)
        return jnp.where(r < last - first, r + first, -1).astype(F32).astype(dtype)

    def assemble(name, down):
        first, last, _, _, rows = GROUPS[name]
        out = None
        for s in range(SIDES):
            hit = row_ids(first, last, BF) == blk_d[s, 0:16]
            hits = [blk_d[s] == BF(a) for a in range(first, last, 2)]
            for p in range(3):
                t = t_parts[p, s]
                z = [jnp.where(h, t, BF(0)) for h in hits]
                z.append(jnp.where(hit, l_parts[p, s], BF(0)))
                if name == "own":
                    z.append(jnp.zeros((16, ELEM), BF))
                d = dot_nt(jnp.concatenate(z, axis=0).astype(F8), onehot[p, s])
                out = d if out is None else out + d
        partial[rows] = out * down

    def fetch(name, down):
        first, last, main, left, rows = GROUPS[name]
        for s in range(SIDES):
            y = dot(table[0, rows], onehot[0, s])
            for p in (1, 2):
                y = y + dot(table[p, rows], onehot[p, s])
            blk = blk_f[s]
            acc = jnp.zeros((3, 8, ELEM), F32)
            for a in range(first, last):
                ya = y[24 * (a - first) : 24 * (a - first) + 24].reshape(3, 8, ELEM)
                acc = jnp.where((blk == F32(a))[None], ya, acc)
            acc = acc.reshape(24, ELEM) * down
            hit = row_ids(first, last, F32).reshape(2, 8, ELEM) == blk[None]
            yl = jnp.where(hit, y[left - main : left - main + 16].reshape(2, 8, ELEM), 0.0)
            acc_left = jnp.sum(yl[0] + yl[1], axis=0, keepdims=True) * down
            if name == "out":
                acc = acc + x_main[s]
                acc_left = acc_left + x_left[s, 0:1]
            x_main[s] = acc
            x_left[s, 0:1] = acc_left

    def gathered():
        rows = [x_main[s] for s in range(SIDES)]
        x = jnp.concatenate([x_left[s, 0:1] for s in range(SIDES)] + [jnp.zeros((10, ELEM), F32)], axis=0)
        x = jnp.concatenate(rows + [x], axis=0)
        hi, lo = split(x)
        x3[0:TP], x3[TP : 2 * TP], x3[2 * TP :] = hi, lo, hi

    def update(name, first):
        rows = GROUPS[name][4]
        step = scale[rows] * partial[rows]
        x = step if first else total[rows] + step
        total[rows] = x
        x_max = largest(x)
        up, down = factors(x_max)
        for p, part in enumerate(split8(x * up)):
            table[p, rows] = part
        return down, x_max

    assemble("out", terms_down)
    pl.semaphore_wait(barrier, 4)
    post(1, partial)
    scale[...] = jnp.zeros_like(scale)
    for a in range(OWN_BLOCKS, BLOCKS):
        diag_block(a)
    post(0, scale)
    for a in range(OWN_BLOCKS):
        diag_block(a)
    assemble("own", terms_down)

    def invert(name):
        rows = GROUPS[name][4]
        d = scale[rows]
        scale[rows] = jnp.where(d == 0.0, 0.0, DAMPING / jnp.where(d == 0.0, 1.0, d))

    invert("own")
    for c in range(ELEM // CHUNK):
        e = slice(c * CHUNK, (c + 1) * CHUNK)
        potential[:, e] = pick(dot(left3[MATS * TP :], src3[:, e]), NP, e)[0:NODES]
    for m in range(MATS):
        hi, lo = split(dot3(split(inv_pad[m]), lift_t, dot_nt))
        w3[NP * m : NP * (m + 1)] = jnp.concatenate([hi, hi, lo], axis=1)
    down, own_max = update("own", True)
    fetch("own", down)
    collect(0, scale)
    collect(1, partial)
    invert("out")
    down, out_max = update("out", True)
    fetch("out", down)

    for sweep in range(SWEEPS - 1):
        gathered()
        terms_up, terms_down = factors(rhs_max + gain * jnp.maximum(own_max, out_max))
        for c in range(ELEM // CHUNK):
            e = slice(c * CHUNK, (c + 1) * CHUNK)
            y = pick(dot(a3[...], x3[:, e]), TP, e)
            store_terms(rhs_terms[:, e] - y, e, terms_up)
        assemble("out", terms_down)
        post(2 + sweep, partial)
        assemble("own", terms_down)
        down, own_max = update("own", False)
        fetch("own", down)
        collect(2 + sweep, partial)
        down, out_max = update("out", False)
        fetch("out", down)

    rows = slice(OWN_MAIN, OWN_LEFT + 16)
    back = jnp.zeros((304, 256), F32)
    for b in range(3):
        cols = slice(256 * b, 256 * (b + 1))
        r = OUT_MAIN + 24 * (b + 3)
        x = total[r : r + 24]
        xl = jnp.broadcast_to(total[OUT_LEFT + b + 3 : OUT_LEFT + b + 4], (16, 256))
        blk = own_blk[:, cols].astype(F32)
        blk2 = (blk - (iota((48, 256), 0) >= 24).astype(F32)).astype(BF)
        hits = [blk2 == BF(a) for a in range(0, OWN_BLOCKS, 2)]
        r16 = iota((16, 256), 0)
        hit = jnp.where(r16 < OWN_BLOCKS, r16, -1).astype(F32).astype(BF) == blk.astype(BF)
        for xv, lv in zip(split(jnp.concatenate([x, x], axis=0)), split(xl)):
            z = jnp.concatenate(
                [jnp.where(h, xv, BF(0)) for h in hits] + [jnp.where(hit, lv, BF(0))], axis=0
            )
            back = back + dot_nt(z, onehot_out[:, cols])
    full = total[rows] + back
    for a in range(OWN_BLOCKS):
        cols = slice(256 * a, 256 * (a + 1))
        trace_own[0:24, cols] = full[24 * a : 24 * a + 24]
        trace_own[24:25, cols] = full[OWN_LEFT + a : OWN_LEFT + a + 1]

    gathered()
    for c in range(ELEM // CHUNK):
        e = slice(c * CHUNK, (c + 1) * CHUNK)
        y = pick(dot(w3[...], x3[:, e]), NP, e)
        potential[:, e] = potential[:, e] - y[0:NODES]

    for r in range(ROUNDS):
        for k in range(4):
            copy(r, k).wait_send()


def shards(source, inverses, lift, stab, material, face_slot, owner_map):
    operands = (
        source,
        inverses.transpose(1, 0, 2),
        lift.T,
        stab.reshape(1, MATS),
        material.reshape(1, ELEM),
        face_slot,
        owner_map,
    )
    vmem = pl.BlockSpec(memory_space=pltpu.VMEM)
    hbm = pl.BlockSpec(memory_space=pltpu.HBM)
    v = pltpu.VMEM
    return pl.pallas_call(
        kernel,
        out_shape=(
            jax.ShapeDtypeStruct((NODES, ELEM), F32),
            jax.ShapeDtypeStruct((FNODES, OWNED), F32),
        ),
        in_specs=[hbm] * 7,
        out_specs=(vmem, vmem),
        scratch_shapes=[
            v((NODES, ELEM), F32),
            v((NODES, MATS, NODES), F32),
            v((SIDES * FNODES, NODES), F32),
            v((1, MATS), F32),
            v((1, ELEM), jnp.int32),
            v((SIDES, ELEM), jnp.int32),
            v((1, GHOSTS), jnp.int32),
            v((3, SIDES, 256, ELEM), F8),
            v((256, GHOSTS), BF),
            v((SIDES, 8, ELEM), F32),
            v((SIDES, 48, ELEM), BF),
            v((SIDES, 16, ELEM), BF),
            v((SIDES, 160, 256), F32),
            v((MATS, NP, NP), F32),
            v((256, NP), F32),
            v((NP, ELEM), F32),
            v((3 * NP, ELEM), BF),
            v((MATS * (TP + NP), 3 * NP), BF),
            v((MATS * TP, 3 * TP), BF),
            v((MATS * NP, 3 * TP), BF),
            v((TP, ELEM), F32),
            v((SIDES, 24, ELEM), F32),
            v((SIDES, 8, ELEM), F32),
            v((3 * TP, ELEM), BF),
            v((3, SIDES, 48, ELEM), BF),
            v((3, SIDES, 16, ELEM), BF),
            v((ROWS, 256), F32),
            v((ROWS, 256), F32),
            v((3, ROWS, 256), F8),
            v((ROWS, 256), F32),
            v((ROUNDS, 2, SENT, CAP_W), F32),
            v((ROUNDS, 2, SENT, CAP_W), F32),
            v((ROUNDS, 2, SENT, CAP_N), F32),
            v((ROUNDS, 2, SENT, CAP_N), F32),
            pltpu.SemaphoreType.DMA((ROUNDS, 4)),
            pltpu.SemaphoreType.DMA((ROUNDS, 4)),
            pltpu.SemaphoreType.DMA((7,)),
        ],
        compiler_params=pltpu.CompilerParams(
            collective_id=0, has_side_effects=True, vmem_limit_bytes=48 * 2**20
        ),
    )(*(pltpu.with_memory_space_constraint(x, pltpu.HBM) for x in operands))


def solution(mesh):
    both = ("wide", "narrow")
    return jax.shard_map(
        shards,
        mesh=mesh,
        in_specs=(
            P(None, both), P(), P(), P(), P(both), P(None, both), P(both, None),
        ),
        out_specs=(P(None, both), P(None, both)),
        check_vma=False,
    )
```

```python
import functools

import jax
import jax.numpy as jnp
from jax import lax
from jax.experimental import pallas as pl
from jax.experimental.pallas import tpu as pltpu
from jax.sharding import PartitionSpec as P

MESH = pl.DeviceIdType.MESH
F32, BF, F8 = jnp.float32, jnp.bfloat16, jnp.float8_e4m3fn
FULL = 3500.0
DAMPING = 0.6
SWEEPS = 3

NODES, FNODES, SIDES, MATS = 125, 25, 6, 4
ELEM = 1024
OWNED = 3 * ELEM
CAP_W, CAP_N = 256, 128
GHOSTS = 2 * CAP_W + 2 * CAP_N
TP = 160
NP = 128

OWN_BLOCKS, BLOCKS = 12, 18
OWN_MAIN, OWN_LEFT, OUT_MAIN, OUT_LEFT, ROWS = 0, 288, 320, 464, 480
GROUPS = {
    "own": (0, 12, OWN_MAIN, OWN_LEFT, slice(0, 320)),
    "out": (12, 18, OUT_MAIN, OUT_LEFT, slice(320, 480)),
}
WEIGHTS = (16.0, 1.0, 0.0625)
SENT = 56
ROUNDS = 2 + SWEEPS - 1


def dot(a, b, precision=None):
    return jnp.dot(a, b, precision=precision, preferred_element_type=F32)


def dot_nt(a, b, precision=None):
    return lax.dot_general(
        a, b, (((1,), (1,)), ((), ())), precision=precision, preferred_element_type=F32
    )


def split(x):
    hi = x.astype(BF)
    return hi, (x - hi.astype(F32)).astype(BF)


def split8(v):
    a = (v * 0.0625).astype(F8)
    r = v - 16.0 * a.astype(F32)
    b = r.astype(F8)
    c = ((r - b.astype(F32)) * 16.0).astype(F8)
    return a, b, c


def dot3(a, b, product):
    return product(a[0], b[0]) + (product(a[0], b[1]) + product(a[1], b[0]))


def largest(x):
    return jnp.max(jnp.max(jnp.abs(x), axis=0, keepdims=True), axis=1, keepdims=True)


def factors(m):
    m = jnp.maximum(m, 1e-30)
    return FULL / m, m * (1.0 / FULL)


def iota(shape, dim):
    return lax.broadcasted_iota(jnp.int32, shape, dim)


def trace_position(p):
    side = jnp.zeros_like(p)
    for i in range(1, SIDES):
        side = side + (p >= 24 * i).astype(jnp.int32)
    node = jnp.where(p < 144, p - 24 * side, 24)
    side = jnp.where(p < 144, side, p - 144)
    return side, node


def kernel(
    source_hbm, inverses_hbm, lift_hbm, stab_hbm, material_hbm, face_slot_hbm, owner_map_hbm,
    potential, trace_own,
    source, inverses, lift, stab, material, face_slot, owner_map,
    onehot, onehot_out, blk_f, blk_d, idx_f, counts,
    inv_pad, lift_pad, src_pad, src3, left3, a3, w3,
    rhs_terms, x_main, x_left, x3, t_parts, l_parts,
    partial, total, table, scale,
    send_w, recv_w, send_n, recv_n, send_sems, recv_sems, in_sems,
):
    loads = [
        pltpu.make_async_copy(src, dst, in_sems.at[i])
        for i, (src, dst) in enumerate(
            (
                (face_slot_hbm, face_slot),
                (owner_map_hbm, owner_map),
                (material_hbm, material),
                (inverses_hbm, inverses),
                (lift_hbm, lift),
                (stab_hbm, stab),
                (source_hbm, source),
            )
        )
    ]
    for load in loads:
        load.start()
    w, n = lax.axis_index("wide"), lax.axis_index("narrow")
    wide, narrow = lax.axis_size("wide"), lax.axis_size("narrow")
    ends = (w == 0, w == wide - 1, n == 0, n == narrow - 1)
    one = (w ^ 1, n ^ 1)
    neighbour = (
        (jnp.where(ends[0], w, w - 1), jnp.where(ends[0], one[1], n)),
        (jnp.where(ends[1], w, w + 1), jnp.where(ends[1], one[1], n)),
        (jnp.where(ends[2], one[0], w), jnp.where(ends[2], n, n - 1)),
        (jnp.where(ends[3], one[0], w), jnp.where(ends[3], n, n + 1)),
    )
    barrier = pltpu.get_barrier_semaphore()
    for k in range(4):
        pl.semaphore_signal(barrier, inc=1, device_id=neighbour[k], device_id_type=MESH)

    def buffers(k):
        return (send_w, recv_w, k) if k < 2 else (send_n, recv_n, k - 2)

    def copy(r, k):
        send, recv, side = buffers(k)
        return pltpu.make_async_remote_copy(
            src_ref=send.at[r, side],
            dst_ref=recv.at[r, jnp.where(ends[k], side, 1 - side)],
            send_sem=send_sems.at[r, k],
            recv_sem=recv_sems.at[r, jnp.where(ends[k], k, k ^ 1)],
            device_id=neighbour[k],
            device_id_type=MESH,
        )

    def arrival(r, k):
        send, recv, side = buffers(k)
        return pltpu.make_async_remote_copy(
            src_ref=send.at[r, side],
            dst_ref=recv.at[r, side],
            send_sem=send_sems.at[r, k],
            recv_sem=recv_sems.at[r, k],
            device_id=neighbour[k],
            device_id_type=MESH,
        )

    def places(k):
        block = min(k, 2)
        lo, width = (0, CAP_W) if k < 2 else ((k - 2) * CAP_N, CAP_N)
        return block, slice(lo, lo + width)

    def post(r, values):
        for k in range(4):
            send, recv, side = buffers(k)
            block, cols = places(k)
            ghost, shared = OUT_MAIN + 24 * block, OUT_MAIN + 24 * (block + 3)
            send[r, side, 0:24] = values[ghost : ghost + 24, cols]
            send[r, side, 24:48] = values[shared : shared + 24, cols]
            ghost, shared = OUT_LEFT + block, OUT_LEFT + block + 3
            send[r, side, 48:49] = values[ghost : ghost + 1, cols]
            send[r, side, 49:50] = values[shared : shared + 1, cols]

            copy(r, k).start()

    def collect(r, values):
        for k in range(4):
            arrival(r, k).wait_recv()

        for k in range(4):
            send, recv, side = buffers(k)
            block, cols = places(k)
            ghost, shared = OUT_MAIN + 24 * block, OUT_MAIN + 24 * (block + 3)
            values[shared : shared + 24, cols] += recv[r, side, 0:24]
            values[ghost : ghost + 24, cols] += recv[r, side, 24:48]
            ghost, shared = OUT_LEFT + block, OUT_LEFT + block + 3
            values[shared : shared + 1, cols] += recv[r, side, 48:49]
            values[ghost : ghost + 1, cols] += recv[r, side, 49:50]

    for load in loads[:3]:
        load.wait()
    owners = owner_map[...]
    own_blk, own_col = owners >> 8, owners & 255
    place = iota((1, GHOSTS), 1) + 1
    onehot_out[...] = (iota((256, GHOSTS), 0) == own_col).astype(F32).astype(BF)
    row16 = iota((16, GHOSTS), 0)
    named = jnp.where(row16 < OWN_BLOCKS, row16, -1) == own_blk
    digits = jnp.concatenate(
        [
            jnp.where(named, (place >> 8).astype(F32), 0.0),
            jnp.where(named, (place & 255).astype(F32), 0.0),
        ],
        axis=0,
    ).astype(BF)
    place_table = dot_nt(digits, onehot_out[...]).astype(BF)

    def renumber(s, carry):
        v = face_slot[pl.ds(s, 1), :]
        row = iota((256, ELEM), 0).astype(F32).astype(BF)
        first = jnp.where(row == (v & 255).astype(F32).astype(BF), BF(1), BF(0))
        found = dot(place_table, first)
        hit = iota((16, ELEM), 0) == (v >> 8)
        spot = jnp.sum(
            jnp.where(hit, 256.0 * found[0:16] + found[16:32], 0.0), axis=0, keepdims=True
        ).astype(jnp.int32)
        v = jnp.where(spot > 0, OWNED + GHOSTS - 1 + spot, v)
        met = row == (v & 255).astype(F32).astype(BF)
        for p, weight in enumerate(WEIGHTS):
            onehot[p, s] = jnp.where(met, BF(weight), BF(0)).astype(F8)
        blk = (v >> 8).astype(F32)
        blk_f[s] = jnp.broadcast_to(blk, (8, ELEM))
        blk_d[s] = (blk - (iota((48, ELEM), 0) >= 24).astype(F32)).astype(BF)
        idx = 8.0 * blk + material[...].astype(F32)
        idx_f[s] = (idx - iota((16, ELEM), 0).astype(F32)).astype(BF)
        return carry

    lax.fori_loop(0, SIDES, renumber, 0, unroll=True)

    def count(s, carry):
        idx = idx_f[s]
        ones = jnp.concatenate(
            [
                jnp.where(idx == BF(16 * t), BF(1), BF(0))
                for t in range(10)
            ],
            axis=0,
        )
        counts[s] = dot_nt(ones.astype(F8), onehot[1, s])
        return carry

    lax.fori_loop(0, SIDES, count, 0, unroll=True)

    for load in loads[3:]:
        load.wait()
    inv_pad[...] = jnp.zeros_like(inv_pad)
    for m in range(MATS):
        inv_pad[m, 0:NODES, 0:NODES] = inverses[:, m, :]
    lift_pad[...] = jnp.zeros_like(lift_pad)
    lift_pad[0 : SIDES * FNODES, 0:NODES] = lift[...]
    src_pad[...] = jnp.zeros_like(src_pad)
    src_pad[0:NODES] = source[...]
    hi, lo = split(src_pad[...])
    src3[0:NP], src3[NP : 2 * NP], src3[2 * NP :] = hi, lo, hi

    side_p, node_p = trace_position(iota((TP, 256), 0))
    order = jnp.where(side_p < SIDES, 6 * node_p + side_p, -1)
    perm = (iota((TP, 256), 1) == order).astype(F32).astype(BF)
    hi, lo = split(lift_pad[...])
    last = (lift_pad[...] - hi.astype(F32) - lo.astype(F32)).astype(BF)
    lift_t = split(dot(perm, hi) + dot(perm, lo) + dot(perm, last))
    row_sum = jnp.zeros((TP, 1), F32)
    eye = iota((TP, TP), 0) == iota((TP, TP), 1)
    col = iota((TP, 192), 1)
    for i in range(1, 4):
        col = col - 48 * (iota((TP, 192), 1) >= 48 * i).astype(jnp.int32)
    side_c, _ = trace_position(iota((TP, 192), 0))
    spread = jnp.zeros((TP, 192), F32)
    for m in range(MATS):
        inv = split(inv_pad[m])
        wt = dot3(lift_t, inv, dot)
        am = dot3(split(wt), lift_t, dot_nt)
        diagonal = jnp.abs(jnp.sum(jnp.where(eye, am, 0.0), axis=1, keepdims=True)) + stab[0:1, m : m + 1]
        spread = spread + jnp.where(col == 8 * side_c + m, diagonal, 0.0)
        am = am + jnp.where(eye, stab[0:1, m : m + 1], 0.0)
        hi, lo = split(am)
        a3[TP * m : TP * (m + 1)] = jnp.concatenate([hi, hi, lo], axis=1)
        row_sum = jnp.maximum(row_sum, jnp.sum(jnp.abs(am), axis=1, keepdims=True))
        hi, lo = split(wt)
        r = slice(TP * m, TP * (m + 1))
        left3[r, 0:NP], left3[r, NP : 2 * NP], left3[r, 2 * NP :] = hi, hi, lo
        hi, lo = inv
        r = slice(MATS * TP + NP * m, MATS * TP + NP * (m + 1))
        left3[r, 0:NP], left3[r, NP : 2 * NP], left3[r, 2 * NP :] = hi, hi, lo
    sdiag = jnp.zeros((24, 192), F32)
    for s in range(SIDES):
        sdiag = sdiag + spread[24 * s : 24 * s + 24]
    last = jnp.sum(spread[144:152], axis=0, keepdims=True)
    sdiag = jnp.concatenate([sdiag, jnp.broadcast_to(last, (8, 192))], axis=0)
    hi = sdiag.astype(BF).astype(F32)
    sdiag = jnp.where(iota((32, 192), 1) < 96, hi, sdiag - hi).astype(BF)

    def diag_block(a):
        _, _, main, left, _ = GROUPS["own" if a < OWN_BLOCKS else "out"]
        b = a if a < OWN_BLOCKS else a - OWN_BLOCKS
        met = jnp.concatenate([counts[s, 8 * a : 8 * a + 8] for s in range(SIDES)], axis=0)
        hi, lo = split(met)
        d = dot(sdiag, jnp.concatenate([hi, lo, hi, lo], axis=0))
        scale[main + 24 * b : main + 24 * b + 24] = d[0:24]
        scale[left + b : left + b + 1] = d[24:25]

    mat = material[...]

    def pick(y, width, e):
        m_row = jnp.broadcast_to(mat[:, e], (8, y.shape[1]))[None]
        y = y.reshape(MATS, width // 8, 8, y.shape[1])
        return jnp.where(
            m_row == 0, y[0], jnp.where(m_row == 1, y[1], jnp.where(m_row == 2, y[2], y[3]))
        ).reshape(width, y.shape[3])

    CHUNK = 512
    for c in range(ELEM // CHUNK):
        e = slice(c * CHUNK, (c + 1) * CHUNK)
        rhs_terms[:, e] = pick(dot(left3[0 : MATS * TP], src3[:, e]), TP, e)

    def store_terms(values, e, up):
        width = values.shape[1]
        for p, part in enumerate(split8(values * up)):
            part = part.astype(F32)
            for s in range(SIDES):
                t = part[24 * s : 24 * s + 24]
                t_parts[p, s, :, e] = jnp.concatenate([t, t], axis=0).astype(BF)
                l = jnp.broadcast_to(part[144 + s : 145 + s], (16, width))
                l_parts[p, s, :, e] = l.astype(BF)

    rhs_max = largest(rhs_terms[...])
    gain = largest(row_sum)
    terms_up, terms_down = factors(rhs_max)
    for c in range(ELEM // CHUNK):
        e = slice(c * CHUNK, (c + 1) * CHUNK)
        store_terms(rhs_terms[:, e], e, terms_up)

    def row_ids(first, last, dtype):
        r = iota((16, ELEM), 0)
        return jnp.where(r < last - first, r + first, -1).astype(F32).astype(dtype)

    def assemble(name, down):
        first, last, _, _, rows = GROUPS[name]
        out = None
        for s in range(SIDES):
            hit = row_ids(first, last, BF) == blk_d[s, 0:16]
            hits = [blk_d[s] == BF(a) for a in range(first, last, 2)]
            for p in range(3):
                t = t_parts[p, s]
                z = [jnp.where(h, t, BF(0)) for h in hits]
                z.append(jnp.where(hit, l_parts[p, s], BF(0)))
                if name == "own":
                    z.append(jnp.zeros((16, ELEM), BF))
                d = dot_nt(jnp.concatenate(z, axis=0).astype(F8), onehot[p, s])
                out = d if out is None else out + d
        partial[rows] = out * down

    def fetch(name, down):
        first, last, main, left, rows = GROUPS[name]
        for s in range(SIDES):
            y = dot(table[0, rows], onehot[0, s])
            for p in (1, 2):
                y = y + dot(table[p, rows], onehot[p, s])
            blk = blk_f[s]
            acc = jnp.zeros((3, 8, ELEM), F32)
            for a in range(first, last):
                ya = y[24 * (a - first) : 24 * (a - first) + 24].reshape(3, 8, ELEM)
                acc = jnp.where((blk == F32(a))[None], ya, acc)
            acc = acc.reshape(24, ELEM) * down
            hit = row_ids(first, last, F32).reshape(2, 8, ELEM) == blk[None]
            yl = jnp.where(hit, y[left - main : left - main + 16].reshape(2, 8, ELEM), 0.0)
            acc_left = jnp.sum(yl[0] + yl[1], axis=0, keepdims=True) * down
            if name == "out":
                acc = acc + x_main[s]
                acc_left = acc_left + x_left[s, 0:1]
            x_main[s] = acc
            x_left[s, 0:1] = acc_left

    def gathered():
        rows = [x_main[s] for s in range(SIDES)]
        x = jnp.concatenate([x_left[s, 0:1] for s in range(SIDES)] + [jnp.zeros((10, ELEM), F32)], axis=0)
        x = jnp.concatenate(rows + [x], axis=0)
        hi, lo = split(x)
        x3[0:TP], x3[TP : 2 * TP], x3[2 * TP :] = hi, lo, hi

    def update(name, first):
        rows = GROUPS[name][4]
        step = scale[rows] * partial[rows]
        x = step if first else total[rows] + step
        total[rows] = x
        x_max = largest(x)
        up, down = factors(x_max)
        for p, part in enumerate(split8(x * up)):
            table[p, rows] = part
        return down, x_max

    assemble("out", terms_down)
    pl.semaphore_wait(barrier, 4)
    post(1, partial)
    scale[...] = jnp.zeros_like(scale)
    for a in range(OWN_BLOCKS, BLOCKS):
        diag_block(a)
    post(0, scale)
    for a in range(OWN_BLOCKS):
        diag_block(a)
    assemble("own", terms_down)

    def invert(name):
        rows = GROUPS[name][4]
        d = scale[rows]
        scale[rows] = jnp.where(d == 0.0, 0.0, DAMPING / jnp.where(d == 0.0, 1.0, d))

    invert("own")
    for c in range(ELEM // CHUNK):
        e = slice(c * CHUNK, (c + 1) * CHUNK)
        potential[:, e] = pick(dot(left3[MATS * TP :], src3[:, e]), NP, e)[0:NODES]
    for m in range(MATS):
        hi, lo = split(dot3(split(inv_pad[m]), lift_t, dot_nt))
        w3[NP * m : NP * (m + 1)] = jnp.concatenate([hi, hi, lo], axis=1)
    down, own_max = update("own", True)
    fetch("own", down)
    collect(0, scale)
    collect(1, partial)
    invert("out")
    down, out_max = update("out", True)
    fetch("out", down)

    for sweep in range(SWEEPS - 1):
        gathered()
        terms_up, terms_down = factors(rhs_max + gain * jnp.maximum(own_max, out_max))
        for c in range(ELEM // CHUNK):
            e = slice(c * CHUNK, (c + 1) * CHUNK)
            y = pick(dot(a3[...], x3[:, e]), TP, e)
            store_terms(rhs_terms[:, e] - y, e, terms_up)
        assemble("out", terms_down)
        post(2 + sweep, partial)
        assemble("own", terms_down)
        down, own_max = update("own", False)
        fetch("own", down)
        collect(2 + sweep, partial)
        down, out_max = update("out", False)
        fetch("out", down)

    rows = slice(OWN_MAIN, OWN_LEFT + 16)
    back = jnp.zeros((304, 256), F32)
    for b in range(3):
        cols = slice(256 * b, 256 * (b + 1))
        r = OUT_MAIN + 24 * (b + 3)
        x = total[r : r + 24]
        xl = jnp.broadcast_to(total[OUT_LEFT + b + 3 : OUT_LEFT + b + 4], (16, 256))
        blk = own_blk[:, cols].astype(F32)
        blk2 = (blk - (iota((48, 256), 0) >= 24).astype(F32)).astype(BF)
        hits = [blk2 == BF(a) for a in range(0, OWN_BLOCKS, 2)]
        r16 = iota((16, 256), 0)
        hit = jnp.where(r16 < OWN_BLOCKS, r16, -1).astype(F32).astype(BF) == blk.astype(BF)
        for xv, lv in zip(split(jnp.concatenate([x, x], axis=0)), split(xl)):
            z = jnp.concatenate(
                [jnp.where(h, xv, BF(0)) for h in hits] + [jnp.where(hit, lv, BF(0))], axis=0
            )
            back = back + dot_nt(z, onehot_out[:, cols])
    full = total[rows] + back
    for a in range(OWN_BLOCKS):
        cols = slice(256 * a, 256 * (a + 1))
        trace_own[0:24, cols] = full[24 * a : 24 * a + 24]
        trace_own[24:25, cols] = full[OWN_LEFT + a : OWN_LEFT + a + 1]

    gathered()
    for c in range(ELEM // CHUNK):
        e = slice(c * CHUNK, (c + 1) * CHUNK)
        y = pick(dot(w3[...], x3[:, e]), NP, e)
        potential[:, e] = potential[:, e] - y[0:NODES]

    for r in range(ROUNDS):
        for k in range(4):
            copy(r, k).wait_send()


def shards(source, inverses, lift, stab, material, face_slot, owner_map):
    operands = (
        source,
        inverses.transpose(1, 0, 2),
        lift.T,
        stab.reshape(1, MATS),
        material.reshape(1, ELEM),
        face_slot,
        owner_map,
    )
    vmem = pl.BlockSpec(memory_space=pltpu.VMEM)
    hbm = pl.BlockSpec(memory_space=pltpu.HBM)
    v = pltpu.VMEM
    return pl.pallas_call(
        kernel,
        out_shape=(
            jax.ShapeDtypeStruct((NODES, ELEM), F32),
            jax.ShapeDtypeStruct((FNODES, OWNED), F32),
        ),
        in_specs=[hbm] * 7,
        out_specs=(vmem, vmem),
        scratch_shapes=[
            v((NODES, ELEM), F32),
            v((NODES, MATS, NODES), F32),
            v((SIDES * FNODES, NODES), F32),
            v((1, MATS), F32),
            v((1, ELEM), jnp.int32),
            v((SIDES, ELEM), jnp.int32),
            v((1, GHOSTS), jnp.int32),
            v((3, SIDES, 256, ELEM), F8),
            v((256, GHOSTS), BF),
            v((SIDES, 8, ELEM), F32),
            v((SIDES, 48, ELEM), BF),
            v((SIDES, 16, ELEM), BF),
            v((SIDES, 160, 256), F32),
            v((MATS, NP, NP), F32),
            v((256, NP), F32),
            v((NP, ELEM), F32),
            v((3 * NP, ELEM), BF),
            v((MATS * (TP + NP), 3 * NP), BF),
            v((MATS * TP, 3 * TP), BF),
            v((MATS * NP, 3 * TP), BF),
            v((TP, ELEM), F32),
            v((SIDES, 24, ELEM), F32),
            v((SIDES, 8, ELEM), F32),
            v((3 * TP, ELEM), BF),
            v((3, SIDES, 48, ELEM), BF),
            v((3, SIDES, 16, ELEM), BF),
            v((ROWS, 256), F32),
            v((ROWS, 256), F32),
            v((3, ROWS, 256), F8),
            v((ROWS, 256), F32),
            v((ROUNDS, 2, SENT, CAP_W), F32),
            v((ROUNDS, 2, SENT, CAP_W), F32),
            v((ROUNDS, 2, SENT, CAP_N), F32),
            v((ROUNDS, 2, SENT, CAP_N), F32),
            pltpu.SemaphoreType.DMA((ROUNDS, 4)),
            pltpu.SemaphoreType.DMA((ROUNDS, 4)),
            pltpu.SemaphoreType.DMA((7,)),
        ],
        compiler_params=pltpu.CompilerParams(
            collective_id=0, has_side_effects=True, vmem_limit_bytes=48 * 2**20
        ),
    )(*(pltpu.with_memory_space_constraint(x, pltpu.HBM) for x in operands))


def solution(mesh):
    both = ("wide", "narrow")
    return jax.shard_map(
        shards,
        mesh=mesh,
        in_specs=(
            P(None, both), P(), P(), P(), P(both), P(None, both), P(both, None),
        ),
        out_specs=(P(None, both), P(None, both)),
        check_vma=False,
    )
```

```python
import functools

import jax
import jax.numpy as jnp
from jax import lax
from jax.experimental import pallas as pl
from jax.experimental.pallas import tpu as pltpu
from jax.sharding import PartitionSpec as P

MESH = pl.DeviceIdType.MESH
F32, BF, F8 = jnp.float32, jnp.bfloat16, jnp.float8_e4m3fn
FULL = 3500.0
DAMPING = 0.6
SWEEPS = 3

NODES, FNODES, SIDES, MATS = 125, 25, 6, 4
ELEM = 1024
OWNED = 3 * ELEM
CAP_W, CAP_N = 256, 128
GHOSTS = 2 * CAP_W + 2 * CAP_N
TP = 160
NP = 128

OWN_BLOCKS, BLOCKS = 12, 18
OWN_MAIN, OWN_LEFT, OUT_MAIN, OUT_LEFT, ROWS = 0, 288, 320, 464, 480
GROUPS = {
    "own": (0, 12, OWN_MAIN, OWN_LEFT, slice(0, 320)),
    "out": (12, 18, OUT_MAIN, OUT_LEFT, slice(320, 480)),
}
WEIGHTS = (16.0, 1.0, 0.0625)
SENT = 56
ROUNDS = 2 + SWEEPS - 1


def dot(a, b, precision=None):
    return jnp.dot(a, b, precision=precision, preferred_element_type=F32)


def dot_nt(a, b, precision=None):
    return lax.dot_general(
        a, b, (((1,), (1,)), ((), ())), precision=precision, preferred_element_type=F32
    )


def split(x):
    hi = x.astype(BF)
    return hi, (x - hi.astype(F32)).astype(BF)


def split8(v):
    a = (v * 0.0625).astype(F8)
    r = v - 16.0 * a.astype(F32)
    b = r.astype(F8)
    c = ((r - b.astype(F32)) * 16.0).astype(F8)
    return a, b, c


def dot3(a, b, product):
    return product(a[0], b[0]) + (product(a[0], b[1]) + product(a[1], b[0]))


def largest(x):
    return jnp.max(jnp.max(jnp.abs(x), axis=0, keepdims=True), axis=1, keepdims=True)


def factors(m):
    m = jnp.maximum(m, 1e-30)
    return FULL / m, m * (1.0 / FULL)


def iota(shape, dim):
    return lax.broadcasted_iota(jnp.int32, shape, dim)


def trace_position(p):
    side = jnp.zeros_like(p)
    for i in range(1, SIDES):
        side = side + (p >= 24 * i).astype(jnp.int32)
    node = jnp.where(p < 144, p - 24 * side, 24)
    side = jnp.where(p < 144, side, p - 144)
    return side, node


def kernel(
    source_hbm, inverses_hbm, lift_hbm, stab_hbm, material_hbm, face_slot_hbm, owner_map_hbm,
    potential, trace_own,
    source, inverses, lift, stab, material, face_slot, owner_map,
    onehot, onehot_out, blk_f, blk_d, idx_f, counts,
    inv_pad, lift_pad, src_pad, src3, left3, a3, w3,
    rhs_terms, x_main, x_left, x3, t_parts, l_parts,
    partial, total, table, scale,
    send_w, recv_w, send_n, recv_n, send_sems, recv_sems, in_sems,
):
    loads = [
        pltpu.make_async_copy(src, dst, in_sems.at[i])
        for i, (src, dst) in enumerate(
            (
                (face_slot_hbm, face_slot),
                (owner_map_hbm, owner_map),
                (material_hbm, material),
                (inverses_hbm, inverses),
                (lift_hbm, lift),
                (stab_hbm, stab),
                (source_hbm, source),
            )
        )
    ]
    for load in loads:
        load.start()
    w, n = lax.axis_index("wide"), lax.axis_index("narrow")
    wide, narrow = lax.axis_size("wide"), lax.axis_size("narrow")
    ends = (w == 0, w == wide - 1, n == 0, n == narrow - 1)
    one = (w ^ 1, n ^ 1)
    neighbour = (
        (jnp.where(ends[0], w, w - 1), jnp.where(ends[0], one[1], n)),
        (jnp.where(ends[1], w, w + 1), jnp.where(ends[1], one[1], n)),
        (jnp.where(ends[2], one[0], w), jnp.where(ends[2], n, n - 1)),
        (jnp.where(ends[3], one[0], w), jnp.where(ends[3], n, n + 1)),
    )
    barrier = pltpu.get_barrier_semaphore()
    for k in range(4):
        pl.semaphore_signal(barrier, inc=1, device_id=neighbour[k], device_id_type=MESH)

    def buffers(k):
        return (send_w, recv_w, k) if k < 2 else (send_n, recv_n, k - 2)

    def copy(r, k):
        send, recv, side = buffers(k)
        return pltpu.make_async_remote_copy(
            src_ref=send.at[r, side],
            dst_ref=recv.at[r, jnp.where(ends[k], side, 1 - side)],
            send_sem=send_sems.at[r, k],
            recv_sem=recv_sems.at[r, jnp.where(ends[k], k, k ^ 1)],
            device_id=neighbour[k],
            device_id_type=MESH,
        )

    def arrival(r, k):
        send, recv, side = buffers(k)
        return pltpu.make_async_remote_copy(
            src_ref=send.at[r, side],
            dst_ref=recv.at[r, side],
            send_sem=send_sems.at[r, k],
            recv_sem=recv_sems.at[r, k],
            device_id=neighbour[k],
            device_id_type=MESH,
        )

    def places(k):
        block = min(k, 2)
        lo, width = (0, CAP_W) if k < 2 else ((k - 2) * CAP_N, CAP_N)
        return block, slice(lo, lo + width)

    def post(r, values):
        for k in range(4):
            send, recv, side = buffers(k)
            block, cols = places(k)
            ghost, shared = OUT_MAIN + 24 * block, OUT_MAIN + 24 * (block + 3)
            send[r, side, 0:24] = values[ghost : ghost + 24, cols]
            send[r, side, 24:48] = values[shared : shared + 24, cols]
            ghost, shared = OUT_LEFT + block, OUT_LEFT + block + 3
            send[r, side, 48:49] = values[ghost : ghost + 1, cols]
            send[r, side, 49:50] = values[shared : shared + 1, cols]

            copy(r, k).start()

    def collect(r, values):
        for k in range(4):
            arrival(r, k).wait_recv()

        for k in range(4):
            send, recv, side = buffers(k)
            block, cols = places(k)
            ghost, shared = OUT_MAIN + 24 * block, OUT_MAIN + 24 * (block + 3)
            values[shared : shared + 24, cols] += recv[r, side, 0:24]
            values[ghost : ghost + 24, cols] += recv[r, side, 24:48]
            ghost, shared = OUT_LEFT + block, OUT_LEFT + block + 3
            values[shared : shared + 1, cols] += recv[r, side, 48:49]
            values[ghost : ghost + 1, cols] += recv[r, side, 49:50]

    for load in loads[:3]:
        load.wait()
    owners = owner_map[...]
    own_blk, own_col = owners >> 8, owners & 255
    place = iota((1, GHOSTS), 1) + 1
    onehot_out[...] = (iota((256, GHOSTS), 0) == own_col).astype(F32).astype(BF)
    row16 = iota((16, GHOSTS), 0)
    named = jnp.where(row16 < OWN_BLOCKS, row16, -1) == own_blk
    digits = jnp.concatenate(
        [
            jnp.where(named, (place >> 8).astype(F32), 0.0),
            jnp.where(named, (place & 255).astype(F32), 0.0),
        ],
        axis=0,
    ).astype(BF)
    place_table = dot_nt(digits, onehot_out[...]).astype(BF)

    def renumber(s, carry):
        v = face_slot[pl.ds(s, 1), :]
        row = iota((256, ELEM), 0).astype(F32).astype(BF)
        first = jnp.where(row == (v & 255).astype(F32).astype(BF), BF(1), BF(0))
        found = dot(place_table, first)
        hit = iota((16, ELEM), 0) == (v >> 8)
        spot = jnp.sum(
            jnp.where(hit, 256.0 * found[0:16] + found[16:32], 0.0), axis=0, keepdims=True
        ).astype(jnp.int32)
        v = jnp.where(spot > 0, OWNED + GHOSTS - 1 + spot, v)
        met = row == (v & 255).astype(F32).astype(BF)
        for p, weight in enumerate(WEIGHTS):
            onehot[p, s] = jnp.where(met, BF(weight), BF(0)).astype(F8)
        blk = (v >> 8).astype(F32)
        blk_f[s] = jnp.broadcast_to(blk, (8, ELEM))
        blk_d[s] = (blk - (iota((48, ELEM), 0) >= 24).astype(F32)).astype(BF)
        idx = 8.0 * blk + material[...].astype(F32)
        idx_f[s] = (idx - iota((16, ELEM), 0).astype(F32)).astype(BF)
        return carry

    lax.fori_loop(0, SIDES, renumber, 0, unroll=True)

    def count(s, carry):
        idx = idx_f[s]
        ones = jnp.concatenate(
            [
                jnp.where(idx == BF(16 * t), BF(1), BF(0))
                for t in range(10)
            ],
            axis=0,
        )
        counts[s] = dot_nt(ones.astype(F8), onehot[1, s])
        return carry

    lax.fori_loop(0, SIDES, count, 0, unroll=True)

    for load in loads[3:]:
        load.wait()
    inv_pad[...] = jnp.zeros_like(inv_pad)
    for m in range(MATS):
        inv_pad[m, 0:NODES, 0:NODES] = inverses[:, m, :]
    lift_pad[...] = jnp.zeros_like(lift_pad)
    lift_pad[0 : SIDES * FNODES, 0:NODES] = lift[...]
    src_pad[...] = jnp.zeros_like(src_pad)
    src_pad[0:NODES] = source[...]
    hi, lo = split(src_pad[...])
    src3[0:NP], src3[NP : 2 * NP], src3[2 * NP :] = hi, lo, hi

    side_p, node_p = trace_position(iota((TP, 256), 0))
    order = jnp.where(side_p < SIDES, 6 * node_p + side_p, -1)
    perm = (iota((TP, 256), 1) == order).astype(F32).astype(BF)
    hi, lo = split(lift_pad[...])
    last = (lift_pad[...] - hi.astype(F32) - lo.astype(F32)).astype(BF)
    lift_t = split(dot(perm, hi) + dot(perm, lo) + dot(perm, last))
    row_sum = jnp.zeros((TP, 1), F32)
    eye = iota((TP, TP), 0) == iota((TP, TP), 1)
    col = iota((TP, 192), 1)
    for i in range(1, 4):
        col = col - 48 * (iota((TP, 192), 1) >= 48 * i).astype(jnp.int32)
    side_c, _ = trace_position(iota((TP, 192), 0))
    spread = jnp.zeros((TP, 192), F32)
    for m in range(MATS):
        inv = split(inv_pad[m])
        wt = dot3(lift_t, inv, dot)
        am = dot3(split(wt), lift_t, dot_nt)
        diagonal = jnp.abs(jnp.sum(jnp.where(eye, am, 0.0), axis=1, keepdims=True)) + stab[0:1, m : m + 1]
        spread = spread + jnp.where(col == 8 * side_c + m, diagonal, 0.0)
        am = am + jnp.where(eye, stab[0:1, m : m + 1], 0.0)
        hi, lo = split(am)
        a3[TP * m : TP * (m + 1)] = jnp.concatenate([hi, hi, lo], axis=1)
        row_sum = jnp.maximum(row_sum, jnp.sum(jnp.abs(am), axis=1, keepdims=True))
        hi, lo = split(wt)
        r = slice(TP * m, TP * (m + 1))
        left3[r, 0:NP], left3[r, NP : 2 * NP], left3[r, 2 * NP :] = hi, hi, lo
        hi, lo = inv
        r = slice(MATS * TP + NP * m, MATS * TP + NP * (m + 1))
        left3[r, 0:NP], left3[r, NP : 2 * NP], left3[r, 2 * NP :] = hi, hi, lo
    sdiag = jnp.zeros((24, 192), F32)
    for s in range(SIDES):
        sdiag = sdiag + spread[24 * s : 24 * s + 24]
    last = jnp.sum(spread[144:152], axis=0, keepdims=True)
    sdiag = jnp.concatenate([sdiag, jnp.broadcast_to(last, (8, 192))], axis=0)
    hi = sdiag.astype(BF).astype(F32)
    sdiag = jnp.where(iota((32, 192), 1) < 96, hi, sdiag - hi).astype(BF)

    def diag_block(a):
        _, _, main, left, _ = GROUPS["own" if a < OWN_BLOCKS else "out"]
        b = a if a < OWN_BLOCKS else a - OWN_BLOCKS
        met = jnp.concatenate([counts[s, 8 * a : 8 * a + 8] for s in range(SIDES)], axis=0)
        hi, lo = split(met)
        d = dot(sdiag, jnp.concatenate([hi, lo, hi, lo], axis=0))
        scale[main + 24 * b : main + 24 * b + 24] = d[0:24]
        scale[left + b : left + b + 1] = d[24:25]

    mat = material[...]

    def pick(y, width, e):
        m_row = jnp.broadcast_to(mat[:, e], (8, y.shape[1]))[None]
        y = y.reshape(MATS, width // 8, 8, y.shape[1])
        return jnp.where(
            m_row == 0, y[0], jnp.where(m_row == 1, y[1], jnp.where(m_row == 2, y[2], y[3]))
        ).reshape(width, y.shape[3])

    CHUNK = 1024
    for c in range(ELEM // CHUNK):
        e = slice(c * CHUNK, (c + 1) * CHUNK)
        rhs_terms[:, e] = pick(dot(left3[0 : MATS * TP], src3[:, e]), TP, e)

    def store_terms(values, e, up):
        width = values.shape[1]
        for p, part in enumerate(split8(values * up)):
            part = part.astype(F32)
            for s in range(SIDES):
                t = part[24 * s : 24 * s + 24]
                t_parts[p, s, :, e] = jnp.concatenate([t, t], axis=0).astype(BF)
                l = jnp.broadcast_to(part[144 + s : 145 + s], (16, width))
                l_parts[p, s, :, e] = l.astype(BF)

    rhs_max = largest(rhs_terms[...])
    gain = largest(row_sum)
    terms_up, terms_down = factors(rhs_max)
    for c in range(ELEM // CHUNK):
        e = slice(c * CHUNK, (c + 1) * CHUNK)
        store_terms(rhs_terms[:, e], e, terms_up)

    def row_ids(first, last, dtype):
        r = iota((16, ELEM), 0)
        return jnp.where(r < last - first, r + first, -1).astype(F32).astype(dtype)

    def assemble(name, down):
        first, last, _, _, rows = GROUPS[name]
        out = None
        for s in range(SIDES):
            hit = row_ids(first, last, BF) == blk_d[s, 0:16]
            hits = [blk_d[s] == BF(a) for a in range(first, last, 2)]
            for p in range(3):
                t = t_parts[p, s]
                z = [jnp.where(h, t, BF(0)) for h in hits]
                z.append(jnp.where(hit, l_parts[p, s], BF(0)))
                if name == "own":
                    z.append(jnp.zeros((16, ELEM), BF))
                d = dot_nt(jnp.concatenate(z, axis=0).astype(F8), onehot[p, s])
                out = d if out is None else out + d
        partial[rows] = out * down

    def fetch(name, down):
        first, last, main, left, rows = GROUPS[name]
        for s in range(SIDES):
            y = dot(table[0, rows], onehot[0, s])
            for p in (1, 2):
                y = y + dot(table[p, rows], onehot[p, s])
            blk = blk_f[s]
            acc = jnp.zeros((3, 8, ELEM), F32)
            for a in range(first, last):
                ya = y[24 * (a - first) : 24 * (a - first) + 24].reshape(3, 8, ELEM)
                acc = jnp.where((blk == F32(a))[None], ya, acc)
            acc = acc.reshape(24, ELEM) * down
            hit = row_ids(first, last, F32).reshape(2, 8, ELEM) == blk[None]
            yl = jnp.where(hit, y[left - main : left - main + 16].reshape(2, 8, ELEM), 0.0)
            acc_left = jnp.sum(yl[0] + yl[1], axis=0, keepdims=True) * down
            if name == "out":
                acc = acc + x_main[s]
                acc_left = acc_left + x_left[s, 0:1]
            x_main[s] = acc
            x_left[s, 0:1] = acc_left

    def gathered():
        rows = [x_main[s] for s in range(SIDES)]
        x = jnp.concatenate([x_left[s, 0:1] for s in range(SIDES)] + [jnp.zeros((10, ELEM), F32)], axis=0)
        x = jnp.concatenate(rows + [x], axis=0)
        hi, lo = split(x)
        x3[0:TP], x3[TP : 2 * TP], x3[2 * TP :] = hi, lo, hi

    def update(name, first):
        rows = GROUPS[name][4]
        step = scale[rows] * partial[rows]
        x = step if first else total[rows] + step
        total[rows] = x
        x_max = largest(x)
        up, down = factors(x_max)
        for p, part in enumerate(split8(x * up)):
            table[p, rows] = part
        return down, x_max

    assemble("out", terms_down)
    pl.semaphore_wait(barrier, 4)
    post(1, partial)
    scale[...] = jnp.zeros_like(scale)
    for a in range(OWN_BLOCKS, BLOCKS):
        diag_block(a)
    post(0, scale)
    for a in range(OWN_BLOCKS):
        diag_block(a)
    assemble("own", terms_down)

    def invert(name):
        rows = GROUPS[name][4]
        d = scale[rows]
        scale[rows] = jnp.where(d == 0.0, 0.0, DAMPING / jnp.where(d == 0.0, 1.0, d))

    invert("own")
    for c in range(ELEM // CHUNK):
        e = slice(c * CHUNK, (c + 1) * CHUNK)
        potential[:, e] = pick(dot(left3[MATS * TP :], src3[:, e]), NP, e)[0:NODES]
    for m in range(MATS):
        hi, lo = split(dot3(split(inv_pad[m]), lift_t, dot_nt))
        w3[NP * m : NP * (m + 1)] = jnp.concatenate([hi, hi, lo], axis=1)
    down, own_max = update("own", True)
    fetch("own", down)
    collect(0, scale)
    collect(1, partial)
    invert("out")
    down, out_max = update("out", True)
    fetch("out", down)

    for sweep in range(SWEEPS - 1):
        gathered()
        terms_up, terms_down = factors(rhs_max + gain * jnp.maximum(own_max, out_max))
        for c in range(ELEM // CHUNK):
            e = slice(c * CHUNK, (c + 1) * CHUNK)
            y = pick(dot(a3[...], x3[:, e]), TP, e)
            store_terms(rhs_terms[:, e] - y, e, terms_up)
        assemble("out", terms_down)
        post(2 + sweep, partial)
        assemble("own", terms_down)
        down, own_max = update("own", False)
        fetch("own", down)
        collect(2 + sweep, partial)
        down, out_max = update("out", False)
        fetch("out", down)

    rows = slice(OWN_MAIN, OWN_LEFT + 16)
    back = jnp.zeros((304, 256), F32)
    for b in range(3):
        cols = slice(256 * b, 256 * (b + 1))
        r = OUT_MAIN + 24 * (b + 3)
        x = total[r : r + 24]
        xl = jnp.broadcast_to(total[OUT_LEFT + b + 3 : OUT_LEFT + b + 4], (16, 256))
        blk = own_blk[:, cols].astype(F32)
        blk2 = (blk - (iota((48, 256), 0) >= 24).astype(F32)).astype(BF)
        hits = [blk2 == BF(a) for a in range(0, OWN_BLOCKS, 2)]
        r16 = iota((16, 256), 0)
        hit = jnp.where(r16 < OWN_BLOCKS, r16, -1).astype(F32).astype(BF) == blk.astype(BF)
        for xv, lv in zip(split(jnp.concatenate([x, x], axis=0)), split(xl)):
            z = jnp.concatenate(
                [jnp.where(h, xv, BF(0)) for h in hits] + [jnp.where(hit, lv, BF(0))], axis=0
            )
            back = back + dot_nt(z, onehot_out[:, cols])
    full = total[rows] + back
    for a in range(OWN_BLOCKS):
        cols = slice(256 * a, 256 * (a + 1))
        trace_own[0:24, cols] = full[24 * a : 24 * a + 24]
        trace_own[24:25, cols] = full[OWN_LEFT + a : OWN_LEFT + a + 1]

    gathered()
    for c in range(ELEM // CHUNK):
        e = slice(c * CHUNK, (c + 1) * CHUNK)
        y = pick(dot(w3[...], x3[:, e]), NP, e)
        potential[:, e] = potential[:, e] - y[0:NODES]

    for r in range(ROUNDS):
        for k in range(4):
            copy(r, k).wait_send()


def shards(source, inverses, lift, stab, material, face_slot, owner_map):
    operands = (
        source,
        inverses.transpose(1, 0, 2),
        lift.T,
        stab.reshape(1, MATS),
        material.reshape(1, ELEM),
        face_slot,
        owner_map,
    )
    vmem = pl.BlockSpec(memory_space=pltpu.VMEM)
    hbm = pl.BlockSpec(memory_space=pltpu.HBM)
    v = pltpu.VMEM
    return pl.pallas_call(
        kernel,
        out_shape=(
            jax.ShapeDtypeStruct((NODES, ELEM), F32),
            jax.ShapeDtypeStruct((FNODES, OWNED), F32),
        ),
        in_specs=[hbm] * 7,
        out_specs=(vmem, vmem),
        scratch_shapes=[
            v((NODES, ELEM), F32),
            v((NODES, MATS, NODES), F32),
            v((SIDES * FNODES, NODES), F32),
            v((1, MATS), F32),
            v((1, ELEM), jnp.int32),
            v((SIDES, ELEM), jnp.int32),
            v((1, GHOSTS), jnp.int32),
            v((3, SIDES, 256, ELEM), F8),
            v((256, GHOSTS), BF),
            v((SIDES, 8, ELEM), F32),
            v((SIDES, 48, ELEM), BF),
            v((SIDES, 16, ELEM), BF),
            v((SIDES, 160, 256), F32),
            v((MATS, NP, NP), F32),
            v((256, NP), F32),
            v((NP, ELEM), F32),
            v((3 * NP, ELEM), BF),
            v((MATS * (TP + NP), 3 * NP), BF),
            v((MATS * TP, 3 * TP), BF),
            v((MATS * NP, 3 * TP), BF),
            v((TP, ELEM), F32),
            v((SIDES, 24, ELEM), F32),
            v((SIDES, 8, ELEM), F32),
            v((3 * TP, ELEM), BF),
            v((3, SIDES, 48, ELEM), BF),
            v((3, SIDES, 16, ELEM), BF),
            v((ROWS, 256), F32),
            v((ROWS, 256), F32),
            v((3, ROWS, 256), F8),
            v((ROWS, 256), F32),
            v((ROUNDS, 2, SENT, CAP_W), F32),
            v((ROUNDS, 2, SENT, CAP_W), F32),
            v((ROUNDS, 2, SENT, CAP_N), F32),
            v((ROUNDS, 2, SENT, CAP_N), F32),
            pltpu.SemaphoreType.DMA((ROUNDS, 4)),
            pltpu.SemaphoreType.DMA((ROUNDS, 4)),
            pltpu.SemaphoreType.DMA((7,)),
        ],
        compiler_params=pltpu.CompilerParams(
            collective_id=0, has_side_effects=True, vmem_limit_bytes=48 * 2**20
        ),
    )(*(pltpu.with_memory_space_constraint(x, pltpu.HBM) for x in operands))


def solution(mesh):
    both = ("wide", "narrow")
    return jax.shard_map(
        shards,
        mesh=mesh,
        in_specs=(
            P(None, both), P(), P(), P(), P(both), P(None, both), P(both, None),
        ),
        out_specs=(P(None, both), P(None, both)),
        check_vma=False,
    )
```
